128 devices in a mesh: seq: 8 (over z_hi, x), wide: 16 (over y, z_lo, core).
Axes of the slice: x: 4, y: 4, z: 4 (z_hi: 2, z_lo: 2; z = z_hi * 2 + z_lo), core: 2. Of those that a mesh axis runs over, the one named last changes fastest.
Arguments:
- queries: bfloat16 [16, 2048, 2048], P('wide', 'seq'), may hold values from -30.284271 to 30.284271
- key_vectors: bfloat16 [16, 2048, 2048], P('wide', 'seq'), may hold values from -6 to 6
- values: bfloat16 [16, 2048, 2048], P('wide', 'seq'), may hold values from -6 to 6
- audio_codes: int32 [16, 2048, 4], P(None, ('seq', 'wide')), may hold values from 0 to 1023
- depth_in: bfloat16 [2048, 1024], replicated, may hold values from -1.25 to 1.25
- code_embed: bfloat16 [3, 1024, 1024], replicated, may hold values from -3 to 3
- norm_gain: float32 [4, 1024], replicated, may hold values from 0.5 to 1.5
- out_heads: bfloat16 [1024, 4, 1024], replicated, may hold values from -0.5 to 0.5
- out_bias: float32 [4, 1024], replicated, may hold values from -330 to 330
Outputs:
- frame_losses: float32 [16, 2048, 4], P(None, ('seq', 'wide'))
- context_grad: bfloat16 [16, 2048, 2048], P('wide', 'seq')
- head_grads: float32 [1024, 4, 1024], P(('seq', 'wide'))
The draws below stay inside these ranges and needn't reach their ends.
All inputs are finite; a program needn't handle non-finite values.
Results may differ from the reference program's by a relative error of at most 0.017.
Values may be sent and summed in bfloat16 or wider, within the bound.
No kernel may reach another device: no remote copies, remote signals or barrier semaphores. Data moves between devices by JAX's collectives and lax.ppermute only.
A program may use at most 192 MiB of HBM per device.

```python
import math
from functools import partial
import jax
import jax.numpy as jnp
import numpy as np
from jax import lax

HEADS = 16
HEAD_DIM = 128
FEATURES = 2048
LENGTH = 2048
GROUPS = 16
DEPTH_DIM = 1024
CODEBOOKS = 4
VOCAB = 1024


def draw_queries(key, part):
    key = jax.random.fold_in(key, 3)
    return jnp.clip(jax.random.normal(key, (GROUPS, LENGTH, FEATURES)), -6.0, 6.0).astype(jnp.bfloat16)


def draw_key_vectors(key, part):
    key = jax.random.fold_in(key, 5)
    return jnp.clip(jax.random.normal(key, (GROUPS, LENGTH, FEATURES)), -6.0, 6.0).astype(jnp.bfloat16)


def draw_out_bias(key, part):
    key = jax.random.fold_in(key, 7)
    first_key = jax.random.fold_in(key, 0)
    return jnp.clip(jax.random.normal(first_key, (CODEBOOKS, VOCAB)), -6.0, 6.0).astype(jnp.float32)


def set_ends(values, stream_key, low, high):
    longest = values.shape.index(max(values.shape))
    spots = []
    for shift in (0, 1):
        where = [jax.random.randint(jax.random.fold_in(stream_key, axis), (), 0, length) for axis, length in enumerate(values.shape)]
        where[longest] = (where[longest] + shift) % values.shape[longest]
        spots.append(tuple(where))
    return values.at[spots[0]].set(low).at[spots[1]].set(high)


def level_of(key, extent, shards, least, top_value):
    loudness = 1.0
    for dim, blocks in shards:
        draws = jax.random.uniform(jax.random.fold_in(jax.random.fold_in(key, 6), dim), (blocks,), jnp.float32, least / len(shards), top_value / len(shards))
        loudness = loudness * jnp.repeat(jnp.exp(draws), extent[dim] // blocks).reshape((-1,) + (1,) * (len(extent) - 1 - dim))
    return loudness


def rank_bounds(number_of, skew):
    loads = [(1 << 20) // math.isqrt(rank ** skew) + 1 for rank in range(1, number_of + 1)]
    scale = 1 + sum(loads) // (1 << 30)
    return np.cumsum(np.array([max(1, weight // scale) for weight in loads]))


def skewed_ids(key, shape, amount, skew):
    listing = rank_bounds(amount, skew)
    pick = jax.random.randint(jax.random.fold_in(key, 1), shape, 0, int(listing[amount - 1]))
    rank = jnp.searchsorted(jnp.asarray(listing, jnp.int32), pick, side="right")
    return jax.random.permutation(jax.random.fold_in(key, 2), amount)[rank].astype(jnp.int32)


def gaussian(key, extent, spread, bound, pieces=(), held_as=jnp.bfloat16):
    entries = spread * jax.random.normal(key, extent, jnp.float32)
    if pieces:
        entries = entries * level_of(key, extent, pieces, -0.22, 0.18)
    return jnp.clip(entries, -bound, bound).astype(held_as)


def setup_inputs(seed: int = 0) -> dict:
    splits = jax.random.split(jax.random.key(seed), 10)
    return {
        "queries": draw_queries(jax.random.fold_in(splits[9], 71), 0),
        "key_vectors": draw_key_vectors(jax.random.fold_in(splits[9], 71), 0),
        "values": gaussian(splits[2], (GROUPS, LENGTH, FEATURES), 1.0, 6.0, ((0, 16), (1, 8))),
        "audio_codes": set_ends(skewed_ids(splits[3], (GROUPS, LENGTH, CODEBOOKS), VOCAB, 2), jax.random.fold_in(splits[3], 3), 0, VOCAB - 1).astype(jnp.int32),
        "depth_in": gaussian(splits[4], (FEATURES, DEPTH_DIM), 0.2, 1.25),
        "code_embed": gaussian(splits[5], (CODEBOOKS - 1, VOCAB, DEPTH_DIM), 0.5, 3.0),
        "norm_gain": jnp.clip(1.0 + 0.1 * jax.random.normal(splits[6], (CODEBOOKS, DEPTH_DIM), jnp.float32), 0.5, 1.5),
        "out_heads": gaussian(splits[7], (DEPTH_DIM, CODEBOOKS, VOCAB), (3.0 / DEPTH_DIM ** 0.5), 0.5),
        "out_bias": draw_out_bias(jax.random.fold_in(splits[9], 71), 0),
    }


def normalize(norm_gain, mixed_in):
    return mixed_in * lax.rsqrt(lax.optimization_barrier(jnp.mean(mixed_in * mixed_in, axis=-1, keepdims=True)) + 1e-05) * norm_gain

def attend_group(group_rows):
    queries, key_vectors, values = group_rows
    block = math.gcd(LENGTH, 512)
    key_heads = key_vectors.reshape(LENGTH, HEADS, HEAD_DIM).astype(jnp.float32)
    value_heads = values.reshape(LENGTH, HEADS, HEAD_DIM).astype(jnp.float32)

    def one_block(block_index):
        first_row = block_index * block
        query_block = lax.dynamic_slice_in_dim(queries, first_row, block, 0)
        query_block = query_block.reshape(block, HEADS, HEAD_DIM).astype(jnp.float32)
        scores = jnp.einsum('qhd,khd->hqk', query_block, key_heads) * HEAD_DIM ** (-0.5)
        query_pos = first_row + jnp.arange(block, dtype=jnp.int32)
        allowed = jnp.arange(LENGTH, dtype=jnp.int32)[None, :] <= query_pos[:, None]
        scores = jnp.where(allowed[None], scores, -jnp.inf)
        top_score = lax.optimization_barrier(jnp.max(scores, axis=2, keepdims=True))
        weights = jnp.exp(scores - top_score)
        weight_sum = lax.optimization_barrier(jnp.sum(weights, axis=2))
        rounded = lax.optimization_barrier(weights.astype(jnp.bfloat16)).astype(jnp.float32)
        summed = jnp.einsum('hqk,khd->qhd', rounded, value_heads)
        return (summed / jnp.transpose(weight_sum)[:, :, None]).reshape(block, FEATURES).astype(jnp.bfloat16)
    blocks = lax.map(one_block, jnp.arange(LENGTH // block, dtype=jnp.int32))
    return blocks.reshape(LENGTH, FEATURES)

def depth_pass(context, targets, depth_in, code_embed, norm_gain, out_heads, out_bias):
    row_count = context.shape[0]
    projected = jnp.dot(context, depth_in, preferred_element_type=jnp.float32)
    looked = code_embed[jnp.arange(CODEBOOKS - 1)[None, :], targets[:, :CODEBOOKS - 1]].astype(jnp.float32)
    mixed_in = projected[:, None, :] + jnp.concatenate((jnp.zeros((row_count, 1, DEPTH_DIM), jnp.float32), looked), axis=1)
    normed, pullback = jax.vjp(partial(normalize, norm_gain), mixed_in)
    hidden = normed.astype(jnp.bfloat16)
    heads_wide = out_heads.astype(jnp.float32)
    logits = jnp.einsum('nce,ecv->ncv', hidden.astype(jnp.float32), heads_wide) + out_bias
    top_logit = lax.optimization_barrier(jnp.max(logits, axis=2, keepdims=True))
    shifted = jnp.exp(logits - top_logit)
    exp_total = lax.optimization_barrier(jnp.sum(shifted, axis=2, keepdims=True))
    onehot = jnp.arange(VOCAB, dtype=jnp.int32)[None, None, :] == targets[:, :, None]
    picked = lax.optimization_barrier(jnp.sum(jnp.where(onehot, logits, 0.0), axis=2))
    losses = top_logit[:, :, 0] + jnp.log(exp_total[:, :, 0]) - picked
    dlogits = (shifted / exp_total - onehot.astype(jnp.float32)).astype(jnp.bfloat16)
    dhidden = jnp.einsum('ncv,ecv->nce', dlogits.astype(jnp.float32), heads_wide)
    dmixed = pullback(dhidden)[0]
    dprojected = lax.optimization_barrier(jnp.sum(dmixed, axis=1)).astype(jnp.bfloat16)
    context_grad = jnp.dot(dprojected, depth_in.T, preferred_element_type=jnp.float32).astype(jnp.bfloat16)
    return (losses, hidden, dlogits, context_grad)

def reference(queries, key_vectors, values, audio_codes, depth_in, code_embed, norm_gain, out_heads, out_bias):
    context = lax.map(attend_group, (queries, key_vectors, values))
    grad_scale = (VOCAB / (GROUPS * LENGTH)) ** 0.5

    def one_group(running, group_items):
        group_context, group_codes = group_items
        losses, hidden, dlogits, context_grad = depth_pass(group_context, group_codes, depth_in, code_embed, norm_gain, out_heads, out_bias)
        partial_sum = jnp.einsum('nce,ncv->ecv', hidden.astype(jnp.float32), dlogits.astype(jnp.float32))
        return (running + partial_sum, (losses, context_grad))
    start_sum = jnp.zeros((DEPTH_DIM, CODEBOOKS, VOCAB), jnp.float32)
    summed, (frame_losses, context_grad) = lax.scan(one_group, start_sum, (context, audio_codes))
    return (frame_losses, context_grad, summed * grad_scale)
```

```python
from functools import partial

import jax
import jax.numpy as jnp
from jax import lax
from jax.experimental import pallas as pl
from jax.experimental.pallas import tpu as pltpu
from jax.sharding import PartitionSpec as P

HEADS = 16
HEAD_DIM = 128
FEATURES = 2048
DEPTH_DIM = 1024
CODEBOOKS = 4
VOCAB = 1024
SEQ = 8
WIDE = 16
FRAMES = 256
LENGTH = SEQ * FRAMES
PAIR = 2 * HEAD_DIM


def attend_kernel(qkv_ref, out_ref):
    to_exp2 = HEAD_DIM ** (-0.5) * 1.4426950408889634
    row = lax.broadcasted_iota(jnp.int32, (FRAMES, FRAMES), 0)
    col = lax.broadcasted_iota(jnp.int32, (FRAMES, FRAMES), 1)
    for head in range(2):
        at = head * HEAD_DIM
        for block in range(SEQ):
            extent = (block + 1) * FRAMES
            first = block * FRAMES
            q = qkv_ref[first:extent, at : at + HEAD_DIM]
            diag = lax.dot_general(
                q,
                qkv_ref[first:extent, PAIR + at : PAIR + at + HEAD_DIM],
                (((1,), (1,)), ((), ())),
                preferred_element_type=jnp.float32,
            )
            diag = jnp.where(col <= row, diag, -jnp.inf)
            top = jnp.max(diag, axis=1, keepdims=True)
            if block:
                past = lax.dot_general(
                    q,
                    qkv_ref[:first, PAIR + at : PAIR + at + HEAD_DIM],
                    (((1,), (1,)), ((), ())),
                    preferred_element_type=jnp.float32,
                )
                top = jnp.maximum(top, jnp.max(past, axis=1, keepdims=True))
            weights = jnp.exp2((diag - top) * to_exp2)
            total = jnp.sum(weights, axis=1, keepdims=True)
            acc = jnp.dot(
                weights.astype(jnp.bfloat16),
                qkv_ref[first:extent, 2 * PAIR + at : 2 * PAIR + at + HEAD_DIM],
                preferred_element_type=jnp.float32,
            )
            if block:
                weights = jnp.exp2((past - top) * to_exp2)
                total = total + jnp.sum(weights, axis=1, keepdims=True)
                acc = acc + jnp.dot(
                    weights.astype(jnp.bfloat16),
                    qkv_ref[:first, 2 * PAIR + at : 2 * PAIR + at + HEAD_DIM],
                    preferred_element_type=jnp.float32,
                )
            out_ref[first:extent, at : at + HEAD_DIM] = (acc / total).astype(jnp.bfloat16)


def attend(qkv):
    return pl.pallas_call(
        attend_kernel,
        out_shape=jax.ShapeDtypeStruct((LENGTH, PAIR), jnp.bfloat16),
        in_specs=[pl.BlockSpec(memory_space=pltpu.VMEM)],
        out_specs=pl.BlockSpec(memory_space=pltpu.VMEM),
        compiler_params=pltpu.CompilerParams(vmem_limit_bytes=40 * 2**20),
        cost_estimate=pl.CostEstimate(
            flops=2 * 36 * FRAMES * FRAMES * HEAD_DIM * 4,
            bytes_accessed=LENGTH * PAIR * 8,
            transcendentals=2 * 36 * FRAMES * FRAMES,
        ),
    )(qkv)


def normalize(norm_gain, mixed_in):
    return (
        mixed_in
        * lax.rsqrt(jnp.mean(mixed_in * mixed_in, axis=-1, keepdims=True) + 1e-05)
        * norm_gain[:, None, :]
    )


def swap_cores(array):
    return lax.ppermute(array, "wide", [(i, i ^ 1) for i in range(WIDE)])


def shards(
    queries, key_vectors, values, audio_codes, depth_in, code_embed, norm_gain, out_heads, out_bias
):
    wide_place = lax.axis_index("wide")
    core = wide_place % 2
    packed = jnp.concatenate(
        [
            a.reshape(FRAMES, SEQ, PAIR).transpose(1, 0, 2)
            for a in (queries[0], key_vectors[0], values[0])
        ],
        axis=2,
    )
    qkv = lax.all_to_all(packed, "seq", 0, 0, tiled=True).reshape(LENGTH, 3 * PAIR)
    codes = lax.all_gather(audio_codes.reshape(WIDE, 64), "wide", axis=0)
    targets = lax.dynamic_index_in_dim(codes, wide_place, 1, keepdims=False).reshape(
        FRAMES, CODEBOOKS
    )
    looked = code_embed[jnp.arange(CODEBOOKS - 1)[:, None], targets.T[: CODEBOOKS - 1]].astype(
        jnp.float32
    )
    heads = out_heads.transpose(1, 0, 2)

    context = attend(qkv).reshape(SEQ, FRAMES, PAIR)
    context = (
        lax.all_to_all(context, "seq", 0, 0, tiled=True)
        .transpose(1, 0, 2)
        .reshape(FRAMES, FEATURES)
    )
    projected = jnp.dot(context, depth_in, preferred_element_type=jnp.float32)
    mixed_in = projected[None] + jnp.concatenate(
        (jnp.zeros((1, FRAMES, DEPTH_DIM), jnp.float32), looked), axis=0
    )
    normed, pullback = jax.vjp(partial(normalize, norm_gain), mixed_in)
    hidden = normed.astype(jnp.bfloat16)
    logits = (
        jnp.einsum("cne,cev->cnv", hidden, heads, preferred_element_type=jnp.float32)
        + out_bias[:, None, :]
    )
    top_logit = jnp.max(logits, axis=2, keepdims=True)
    shifted = jnp.exp(logits - top_logit)
    exp_total = jnp.sum(shifted, axis=2, keepdims=True)
    onehot = jnp.arange(VOCAB, dtype=jnp.int32)[None, None, :] == targets.T[:, :, None]
    picked = jnp.sum(jnp.where(onehot, logits, 0.0), axis=2)
    losses = top_logit[:, :, 0] + jnp.log(exp_total[:, :, 0]) - picked
    dlogits = (shifted / exp_total - onehot.astype(jnp.float32)).astype(jnp.bfloat16)

    mine = 2 * core
    other = 2 - mine

    def pair(array):
        theirs = swap_cores(lax.dynamic_slice_in_dim(array, other, 2, 0))
        return jnp.concatenate((lax.dynamic_slice_in_dim(array, mine, 2, 0), theirs), axis=1)

    partial_grads = jnp.einsum(
        "cne,cnv->ecv", pair(hidden), pair(dlogits), preferred_element_type=jnp.float32
    ).astype(jnp.bfloat16)
    shares = lax.all_to_all(
        partial_grads.reshape(SEQ * WIDE, 8, 2, VOCAB), ("seq", "wide"), 0, 0, tiled=True
    )
    grad_scale = (VOCAB / (SEQ * WIDE * FRAMES)) ** 0.5
    summed = jnp.sum(shares.reshape(SEQ * WIDE // 2, 2, 8, 2, VOCAB).astype(jnp.float32), axis=0)
    head_grads = summed.transpose(1, 0, 2, 3).reshape(8, CODEBOOKS, VOCAB) * grad_scale

    dhidden = jnp.einsum("cnv,cev->cne", dlogits, heads, preferred_element_type=jnp.float32)
    dmixed = pullback(dhidden)[0]
    dprojected = jnp.sum(dmixed, axis=0).astype(jnp.bfloat16)
    context_grad = lax.dot_general(
        dprojected, depth_in, (((1,), (1,)), ((), ())), preferred_element_type=jnp.float32
    ).astype(jnp.bfloat16)

    all_losses = lax.all_gather(losses.T.reshape(WIDE, 64), "wide", axis=0)
    frame_losses = lax.dynamic_index_in_dim(all_losses, wide_place, 1, keepdims=False).reshape(
        WIDE, 16, CODEBOOKS
    )
    return (frame_losses, context_grad.reshape(1, FRAMES, FEATURES), head_grads)


def solution(mesh):
    return jax.shard_map(
        shards,
        mesh=mesh,
        in_specs=(
            P("wide", "seq", None),
            P("wide", "seq", None),
            P("wide", "seq", None),
            P(None, ("seq", "wide"), None),
            P(),
            P(),
            P(),
            P(),
            P(),
        ),
        out_specs=(
            P(None, ("seq", "wide"), None),
            P("wide", "seq", None),
            P(("seq", "wide"), None, None),
        ),
        check_vma=False,
    )
```

```python
from functools import partial

import jax
import jax.numpy as jnp
from jax import lax
from jax.experimental import pallas as pl
from jax.experimental.pallas import tpu as pltpu
from jax.sharding import PartitionSpec as P

HEADS = 16
HEAD_DIM = 128
FEATURES = 2048
DEPTH_DIM = 1024
CODEBOOKS = 4
VOCAB = 1024
SEQ = 8
WIDE = 16
FRAMES = 256
LENGTH = SEQ * FRAMES
PAIR = 2 * HEAD_DIM


def attend_kernel(qkv_ref, out_ref):
    to_exp2 = HEAD_DIM ** (-0.5) * 1.4426950408889634
    row = lax.broadcasted_iota(jnp.int32, (FRAMES, FRAMES), 0)
    col = lax.broadcasted_iota(jnp.int32, (FRAMES, FRAMES), 1)
    for head in range(2):
        at = head * HEAD_DIM
        for block in range(SEQ):
            extent = (block + 1) * FRAMES
            first = block * FRAMES
            q = qkv_ref[first:extent, at : at + HEAD_DIM]
            diag = lax.dot_general(
                q,
                qkv_ref[first:extent, PAIR + at : PAIR + at + HEAD_DIM],
                (((1,), (1,)), ((), ())),
                preferred_element_type=jnp.float32,
            )
            diag = jnp.where(col <= row, diag, -jnp.inf)
            top = jnp.max(diag, axis=1, keepdims=True)
            if block:
                past = lax.dot_general(
                    q,
                    qkv_ref[:first, PAIR + at : PAIR + at + HEAD_DIM],
                    (((1,), (1,)), ((), ())),
                    preferred_element_type=jnp.float32,
                )
                top = jnp.maximum(top, jnp.max(past, axis=1, keepdims=True))
            weights = jnp.exp2((diag - top) * to_exp2)
            total = jnp.sum(weights, axis=1, keepdims=True)
            acc = jnp.dot(
                weights.astype(jnp.bfloat16),
                qkv_ref[first:extent, 2 * PAIR + at : 2 * PAIR + at + HEAD_DIM],
                preferred_element_type=jnp.float32,
            )
            if block:
                weights = jnp.exp2((past - top) * to_exp2)
                total = total + jnp.sum(weights, axis=1, keepdims=True)
                acc = acc + jnp.dot(
                    weights.astype(jnp.bfloat16),
                    qkv_ref[:first, 2 * PAIR + at : 2 * PAIR + at + HEAD_DIM],
                    preferred_element_type=jnp.float32,
                )
            out_ref[block, :, at : at + HEAD_DIM] = (acc / total).astype(jnp.bfloat16)


def attend(qkv):
    return pl.pallas_call(
        attend_kernel,
        out_shape=jax.ShapeDtypeStruct((SEQ, FRAMES, PAIR), jnp.bfloat16),
        in_specs=[pl.BlockSpec(memory_space=pltpu.VMEM)],
        out_specs=pl.BlockSpec(memory_space=pltpu.VMEM),
        compiler_params=pltpu.CompilerParams(vmem_limit_bytes=40 * 2**20),
        cost_estimate=pl.CostEstimate(
            flops=2 * 36 * FRAMES * FRAMES * HEAD_DIM * 4,
            bytes_accessed=LENGTH * PAIR * 8,
            transcendentals=2 * 36 * FRAMES * FRAMES,
        ),
    )(qkv)


def pack_kernel(queries, key_vectors, values, out):
    for kind, ref in enumerate((queries, key_vectors, values)):
        out[0, :, kind * PAIR : (kind + 1) * PAIR] = ref[0]


def pack(queries, key_vectors, values):
    return pl.pallas_call(
        pack_kernel,
        grid=(SEQ,),
        out_shape=jax.ShapeDtypeStruct((SEQ, FRAMES, 3 * PAIR), jnp.bfloat16),
        in_specs=[pl.BlockSpec((1, FRAMES, PAIR), lambda i: (0, 0, i))] * 3,
        out_specs=pl.BlockSpec((1, FRAMES, 3 * PAIR), lambda i: (i, 0, 0)),
        cost_estimate=pl.CostEstimate(flops=0, bytes_accessed=6 * 2**20, transcendentals=0),
    )(queries, key_vectors, values)


def depth_head(projected, embed, gain, heads, bias, target):
    mixed = projected + embed.astype(jnp.float32)
    scale = lax.rsqrt(jnp.mean(mixed * mixed, axis=1, keepdims=True) + 1e-05)
    hidden = (mixed * scale * gain).astype(jnp.bfloat16)
    logits = jnp.dot(hidden, heads, preferred_element_type=jnp.float32) + bias
    top = jnp.max(logits, axis=1, keepdims=True)
    shifted = jnp.exp(logits - top)
    total = jnp.sum(shifted, axis=1, keepdims=True)
    onehot = lax.broadcasted_iota(jnp.int32, (FRAMES, VOCAB), 1) == target
    picked = jnp.sum(jnp.where(onehot, logits, 0.0), axis=1, keepdims=True)
    losses = top + jnp.log(total) - picked
    dlogits = (shifted / total - onehot.astype(jnp.float32)).astype(jnp.bfloat16)
    return hidden, dlogits, losses


def depth_kernel(first, book, *refs):
    if first:
        (ctx_hbm, depth_hbm, embed_hbm, heads_hbm, gain, bias, target) = refs[:7]
        (projected, acts, losses, ctx, depth_in, embed, heads, sems) = refs[7:]
    else:
        (projected, embed_hbm, heads_hbm, gain, bias, target) = refs[:6]
        (acts, losses, embed, heads, sems) = refs[6:]
    copies = []

    def fetch(source, target_ref):
        copy = pltpu.make_async_copy(source, target_ref, sems.at[len(copies)])
        copy.start()
        copies.append(copy)
        return copy

    pieces = 4
    rows = FEATURES // pieces
    if first:
        ctx_copy = fetch(ctx_hbm, ctx)
        depth_copies = [
            fetch(
                depth_hbm.at[i * rows : (i + 1) * rows], depth_in.at[i * rows : (i + 1) * rows]
            )
            for i in range(pieces)
        ]
    book_copies = [
        (fetch(embed_hbm.at[book[0] + j], embed.at[j]), fetch(heads_hbm.at[book[0] + j], heads.at[j]))
        for j in range(2)
    ]
    if first:
        ctx_copy.wait()
        total = None
        for i in range(pieces):
            depth_copies[i].wait()
            for part in range(i * SEQ // pieces, (i + 1) * SEQ // pieces):
                term = jnp.dot(
                    ctx[part],
                    depth_in[part * PAIR : (part + 1) * PAIR],
                    preferred_element_type=jnp.float32,
                )
                total = term if total is None else total + term
        projected[...] = total
    lane = lax.broadcasted_iota(jnp.int32, (FRAMES, CODEBOOKS), 1)
    both = []
    for j in range(2):
        c = book[0] + j
        for copy in book_copies[j]:
            copy.wait()
        token = jnp.sum(jnp.where(lane == c, target[...], 0), axis=1, keepdims=True)
        hidden, dlogits, loss = depth_head(
            projected[...], embed[j], gain[c], heads[j], bias[c], token
        )
        acts[0, j] = hidden
        acts[1, j] = dlogits
        both.append(loss)
    pair_lane = lax.broadcasted_iota(jnp.int32, (FRAMES, 2), 1)
    losses[...] = jnp.where(pair_lane == 0, both[0], both[1])


def depth_call(first, outs, book, hbm_args, vmem_args):
    vmem = pl.BlockSpec(memory_space=pltpu.VMEM)
    anywhere = pl.BlockSpec(memory_space=pl.ANY)
    scratch = [
        pltpu.VMEM((2, FRAMES, DEPTH_DIM), jnp.bfloat16),
        pltpu.VMEM((2, DEPTH_DIM, VOCAB), jnp.bfloat16),
        pltpu.SemaphoreType.DMA((9 if first else 4,)),
    ]
    if first:
        scratch = [
            pltpu.VMEM((SEQ, FRAMES, PAIR), jnp.bfloat16),
            pltpu.VMEM((FEATURES, DEPTH_DIM), jnp.bfloat16),
        ] + scratch
    in_specs = [anywhere] * len(hbm_args) + [vmem] * len(vmem_args)
    if not first:
        in_specs[0] = vmem
    return pl.pallas_call(
        partial(depth_kernel, first),
        out_shape=outs,
        in_specs=[pl.BlockSpec(memory_space=pltpu.SMEM)] + in_specs,
        out_specs=(vmem,) * len(outs),
        scratch_shapes=scratch,
        compiler_params=pltpu.CompilerParams(vmem_limit_bytes=40 * 2**20),
        cost_estimate=pl.CostEstimate(
            flops=2 * 2 * FRAMES * DEPTH_DIM * VOCAB,
            bytes_accessed=8 * 2**20,
            transcendentals=2 * FRAMES * VOCAB,
        ),
    )(book.reshape(1), *hbm_args, *vmem_args)


def outer_kernel(mine, theirs, out):
    chunk = 128
    at = pl.multiple_of(pl.program_id(0) * chunk, chunk)
    both = []
    for j in range(2):
        total = None
        for acts in (mine, theirs):
            term = lax.dot_general(
                acts[0, j, :, pl.ds(at, chunk)],
                acts[1, j],
                (((0,), (0,)), ((), ())),
                preferred_element_type=jnp.float32,
            )
            total = term if total is None else total + term
        both.append(total.reshape(chunk // 8, 8, VOCAB))
    out[...] = jnp.concatenate(both, axis=1).astype(jnp.bfloat16)


def outer(mine, theirs):
    vmem = pl.BlockSpec(memory_space=pltpu.VMEM)
    return pl.pallas_call(
        outer_kernel,
        grid=(8,),
        out_shape=jax.ShapeDtypeStruct((SEQ * WIDE, 16, VOCAB), jnp.bfloat16),
        in_specs=[vmem] * 2,
        out_specs=pl.BlockSpec((16, 16, VOCAB), lambda i: (i, 0, 0)),
        compiler_params=pltpu.CompilerParams(vmem_limit_bytes=40 * 2**20),
        cost_estimate=pl.CostEstimate(
            flops=2 * 2 * 2 * FRAMES * DEPTH_DIM * VOCAB,
            bytes_accessed=8 * 2**20,
            transcendentals=0,
        ),
    )(mine, theirs)


def normalize(norm_gain, mixed_in):
    return (
        mixed_in
        * lax.rsqrt(jnp.mean(mixed_in * mixed_in, axis=-1, keepdims=True) + 1e-05)
        * norm_gain[:, None, :]
    )


def swap_wide(array, stride):
    return lax.ppermute(array, "wide", [(i, i ^ stride) for i in range(WIDE)])


def share_out(rows):
    place = lax.axis_index("wide")
    held = rows.reshape(2, 2, 2, 2, rows.shape[1])
    for axis, stride in enumerate((8, 4, 2, 1)):
        high = (place // stride) % 2 == 1
        low_part = lax.index_in_dim(held, 0, axis, keepdims=True)
        high_part = lax.index_in_dim(held, 1, axis, keepdims=True)
        kept = jnp.where(high, high_part, low_part)
        came = swap_wide(jnp.where(high, low_part, high_part), stride)
        held = jnp.concatenate(
            (jnp.where(high, came, kept), jnp.where(high, kept, came)), axis=axis
        )
    return held.reshape(WIDE, rows.shape[1])


def shards(
    queries, key_vectors, values, audio_codes, depth_in, code_embed, norm_gain, out_heads, out_bias
):
    core = lax.axis_index("wide") % 2
    qkv = lax.all_to_all(pack(queries, key_vectors, values), "seq", 0, 0, tiled=True)
    targets = share_out(audio_codes.reshape(WIDE, 64)).reshape(FRAMES, CODEBOOKS).T
    chosen = jnp.arange(VOCAB, dtype=jnp.int32) == targets[: CODEBOOKS - 1, :, None]
    looked = jnp.einsum(
        "cnv,cve->cne",
        chosen.astype(jnp.bfloat16),
        code_embed,
        preferred_element_type=jnp.float32,
    ).astype(jnp.bfloat16)
    looked = jnp.concatenate((jnp.zeros((1, FRAMES, DEPTH_DIM), jnp.bfloat16), looked), axis=0)
    heads = out_heads.transpose(1, 0, 2)
    qkv, looked, heads = lax.optimization_barrier((qkv, looked, heads))
    small = (norm_gain[:, None, :], out_bias[:, None, :], targets.T)

    context = lax.all_to_all(
        attend(qkv.reshape(LENGTH, 3 * PAIR)), "seq", 0, 0, tiled=True
    )
    mine = 2 * core
    other = 2 - mine
    acts_shape = jax.ShapeDtypeStruct((2, 2, FRAMES, DEPTH_DIM), jnp.bfloat16)
    losses_shape = jax.ShapeDtypeStruct((FRAMES, 2), jnp.float32)
    projected, acts_other, losses_other = depth_call(
        True,
        (jax.ShapeDtypeStruct((FRAMES, DEPTH_DIM), jnp.float32), acts_shape, losses_shape),
        other,
        (context, depth_in, looked, heads),
        small,
    )
    came = swap_wide(acts_other, 1)
    acts_mine, losses_mine = depth_call(
        False, (acts_shape, losses_shape), mine, (projected, looked, heads), small
    )
    shares = lax.all_to_all(outer(acts_mine, came), ("seq", "wide"), 0, 0, tiled=True)
    grad_scale = (VOCAB / (SEQ * WIDE * FRAMES)) ** 0.5
    summed = jnp.sum(shares.reshape(SEQ * WIDE // 2, 4, 8, VOCAB).astype(jnp.float32), axis=0)
    head_grads = summed.transpose(1, 0, 2) * grad_scale

    def in_order(of_mine, of_other):
        low = jnp.where(core == 0, of_mine, of_other)
        high = jnp.where(core == 0, of_other, of_mine)
        return jnp.concatenate((low, high), axis=0)

    dlogits = in_order(acts_mine[1], acts_other[1])
    pullback = jax.vjp(
        partial(normalize, norm_gain), projected[None] + looked.astype(jnp.float32)
    )[1]
    dhidden = jnp.einsum("cnv,cev->cne", dlogits, heads, preferred_element_type=jnp.float32)
    dmixed = pullback(dhidden)[0]
    dprojected = jnp.sum(dmixed, axis=0).astype(jnp.bfloat16)
    context_grad = lax.dot_general(
        dprojected, depth_in, (((1,), (1,)), ((), ())), preferred_element_type=jnp.float32
    ).astype(jnp.bfloat16)
    losses = jnp.where(
        core == 0,
        jnp.concatenate((losses_mine, losses_other), axis=1),
        jnp.concatenate((losses_other, losses_mine), axis=1),
    )
    losses, context_grad = lax.optimization_barrier((losses, context_grad))
    frame_losses = share_out(losses.reshape(WIDE, 64)).reshape(WIDE, 16, CODEBOOKS)
    return (frame_losses, context_grad.reshape(1, FRAMES, FEATURES), head_grads)


def solution(mesh):
    return jax.shard_map(
        shards,
        mesh=mesh,
        in_specs=(
            P("wide", "seq", None),
            P("wide", "seq", None),
            P("wide", "seq", None),
            P(None, ("seq", "wide"), None),
            P(),
            P(),
            P(),
            P(),
            P(),
        ),
        out_specs=(
            P(None, ("seq", "wide"), None),
            P("wide", "seq", None),
            P(("seq", "wide"), None, None),
        ),
        check_vma=False,
    )
```

```python
from functools import partial

import jax
import jax.numpy as jnp
from jax import lax
from jax.experimental import pallas as pl
from jax.experimental.pallas import tpu as pltpu
from jax.sharding import PartitionSpec as P

HEADS = 16
HEAD_DIM = 128
FEATURES = 2048
DEPTH_DIM = 1024
CODEBOOKS = 4
VOCAB = 1024
SEQ = 8
WIDE = 16
FRAMES = 256
LENGTH = SEQ * FRAMES
PAIR = 2 * HEAD_DIM


def attend_kernel(qkv, out_hbm, out, out_sems):
    stores = [
        pltpu.make_async_copy(out.at[i], out_hbm.at[i], out_sems.at[i]) for i in range(SEQ)
    ]
    to_exp2 = HEAD_DIM ** (-0.5) * 1.4426950408889634
    row = lax.broadcasted_iota(jnp.int32, (FRAMES, FRAMES), 0)
    col = lax.broadcasted_iota(jnp.int32, (FRAMES, FRAMES), 1)
    across = (((1,), (1,)), ((), ()))
    for block in range(SEQ):
        for head in range(2):
            at = head * HEAD_DIM
            q = qkv[block, :, at : at + HEAD_DIM]
            diag = lax.dot_general(
                q,
                qkv[block, :, PAIR + at : PAIR + at + HEAD_DIM],
                across,
                preferred_element_type=jnp.float32,
            )
            diag = jnp.where(col <= row, diag, -jnp.inf)
            top = jnp.max(diag, axis=1, keepdims=True)
            if block:
                keys = qkv[:block, :, PAIR + at : PAIR + at + HEAD_DIM]
                past = lax.dot_general(
                    q,
                    keys.reshape(block * FRAMES, HEAD_DIM),
                    across,
                    preferred_element_type=jnp.float32,
                )
                top = jnp.maximum(top, jnp.max(past, axis=1, keepdims=True))
            weights = jnp.exp2((diag - top) * to_exp2)
            total = jnp.sum(weights, axis=1, keepdims=True)
            acc = jnp.dot(
                weights.astype(jnp.bfloat16),
                qkv[block, :, 2 * PAIR + at : 2 * PAIR + at + HEAD_DIM],
                preferred_element_type=jnp.float32,
            )
            if block:
                weights = jnp.exp2((past - top) * to_exp2)
                total = total + jnp.sum(weights, axis=1, keepdims=True)
                vals = qkv[:block, :, 2 * PAIR + at : 2 * PAIR + at + HEAD_DIM]
                acc = acc + jnp.dot(
                    weights.astype(jnp.bfloat16),
                    vals.reshape(block * FRAMES, HEAD_DIM),
                    preferred_element_type=jnp.float32,
                )
            out[block, :, at : at + HEAD_DIM] = (acc / total).astype(jnp.bfloat16)
        stores[block].start()
    for copy in stores:
        copy.wait()


HBM = pl.BlockSpec(memory_space=pltpu.HBM)
VMEM = pl.BlockSpec(memory_space=pltpu.VMEM)
SMEM = pl.BlockSpec(memory_space=pltpu.SMEM)
GRANT = 60 * 2**20
DEPTH_GRANT = 50 * 2**20


def attend(qkv):
    return pl.pallas_call(
        attend_kernel,
        out_shape=pltpu.HBM((SEQ, FRAMES, PAIR), jnp.bfloat16),
        in_specs=[VMEM],
        out_specs=HBM,
        scratch_shapes=[
            pltpu.VMEM((SEQ, FRAMES, PAIR), jnp.bfloat16),
            pltpu.SemaphoreType.DMA((SEQ,)),
        ],
        compiler_params=pltpu.CompilerParams(vmem_limit_bytes=40 * 2**20),
        cost_estimate=pl.CostEstimate(
            flops=2 * 36 * FRAMES * FRAMES * HEAD_DIM * 4,
            bytes_accessed=LENGTH * PAIR * 8,
            transcendentals=2 * 36 * FRAMES * FRAMES,
        ),
    )(qkv)


def pack_kernel(queries, key_vectors, values, out, held, in_sems, out_sems):
    rows = FRAMES // 4
    sources = (queries, key_vectors, values)
    loads = [
        [
            pltpu.make_async_copy(
                ref.at[0, i * rows : (i + 1) * rows],
                held.at[kind, i * rows : (i + 1) * rows],
                in_sems.at[i, kind],
            )
            for kind, ref in enumerate(sources)
        ]
        for i in range(4)
    ]
    for group in loads:
        for copy in group:
            copy.start()
    stores = []
    for i in range(4):
        for kind in range(3):
            loads[i][kind].wait()
            for part in range(SEQ):
                copy = pltpu.make_async_copy(
                    held.at[kind, i * rows : (i + 1) * rows, part * PAIR : (part + 1) * PAIR],
                    out.at[part, i * rows : (i + 1) * rows, kind * PAIR : (kind + 1) * PAIR],
                    out_sems.at[i, kind, part],
                )
                copy.start()
                stores.append(copy)
    for copy in stores:
        copy.wait()


def pack(queries, key_vectors, values):
    return pl.pallas_call(
        pack_kernel,
        out_shape=pltpu.HBM((SEQ, FRAMES, 3 * PAIR), jnp.bfloat16),
        in_specs=[HBM] * 3,
        out_specs=HBM,
        scratch_shapes=[
            pltpu.VMEM((3, FRAMES, FEATURES), jnp.bfloat16),
            pltpu.SemaphoreType.DMA((4, 3)),
            pltpu.SemaphoreType.DMA((4, 3, SEQ)),
        ],
        compiler_params=pltpu.CompilerParams(vmem_limit_bytes=GRANT),
        cost_estimate=pl.CostEstimate(flops=0, bytes_accessed=6 * 2**20, transcendentals=0),
    )(queries, key_vectors, values)


def lookup_kernel(target, table_hbm, out_hbm, table, out, in_sems, out_sems):
    books = CODEBOOKS - 1
    loads = [
        pltpu.make_async_copy(table_hbm.at[c], table.at[c], in_sems.at[c]) for c in range(books)
    ]
    stores = [
        pltpu.make_async_copy(out.at[c], out_hbm.at[c], out_sems.at[c])
        for c in range(CODEBOOKS)
    ]
    for copy in loads:
        copy.start()
    out[0] = jnp.zeros((FRAMES, DEPTH_DIM), jnp.bfloat16)
    stores[0].start()
    for c in range(books):
        loads[c].wait()
        chosen = lax.broadcasted_iota(jnp.int32, (FRAMES, VOCAB), 1) == target[:, c : c + 1]
        out[c + 1] = jnp.dot(
            chosen.astype(jnp.float32).astype(jnp.bfloat16),
            table[c],
            preferred_element_type=jnp.float32,
        ).astype(jnp.bfloat16)
        stores[c + 1].start()
    for copy in stores:
        copy.wait()


def lookup(target, table):
    return pl.pallas_call(
        lookup_kernel,
        out_shape=pltpu.HBM((CODEBOOKS, FRAMES, DEPTH_DIM), jnp.bfloat16),
        in_specs=[VMEM, HBM],
        out_specs=HBM,
        scratch_shapes=[
            pltpu.VMEM((CODEBOOKS - 1, VOCAB, DEPTH_DIM), jnp.bfloat16),
            pltpu.VMEM((CODEBOOKS, FRAMES, DEPTH_DIM), jnp.bfloat16),
            pltpu.SemaphoreType.DMA((CODEBOOKS - 1,)),
            pltpu.SemaphoreType.DMA((CODEBOOKS,)),
        ],
        compiler_params=pltpu.CompilerParams(vmem_limit_bytes=40 * 2**20),
        cost_estimate=pl.CostEstimate(
            flops=6 * FRAMES * VOCAB * DEPTH_DIM, bytes_accessed=8 * 2**20, transcendentals=0
        ),
    )(target, table)


def depth_head(projected, embed, gain, heads, bias, target):
    mixed = projected + embed.astype(jnp.float32)
    scale = lax.rsqrt(jnp.mean(mixed * mixed, axis=1, keepdims=True) + 1e-05)
    hidden = (mixed * scale * gain).astype(jnp.bfloat16)
    logits = jnp.dot(hidden, heads, preferred_element_type=jnp.float32) + bias
    top = jnp.max(logits, axis=1, keepdims=True)
    shifted = jnp.exp(logits - top)
    total = jnp.sum(shifted, axis=1, keepdims=True)
    onehot = lax.broadcasted_iota(jnp.int32, (FRAMES, VOCAB), 1) == target
    picked = jnp.sum(jnp.where(onehot, logits, 0.0), axis=1, keepdims=True)
    losses = top + jnp.log(total) - picked
    dlogits = (shifted / total - onehot.astype(jnp.float32)).astype(jnp.bfloat16)
    return hidden, dlogits, losses


def depth_kernel(first, book, *refs):
    if first:
        (ctx_hbm, depth_hbm, embed_hbm, heads_hbm, gain, bias, target) = refs[:7]
        (projected, acts_hbm, losses, acts, ctx, depth_in, embed, heads, sems) = refs[7:]
    else:
        (projected, embed_hbm, heads_hbm, gain, bias, target) = refs[:6]
        (acts, losses, embed, heads, sems) = refs[6:]
    count = [0]

    def fetch(source, kept, pieces):
        rows = kept.shape[0] // pieces
        copies = []
        for i in range(pieces):
            here = slice(i * rows, (i + 1) * rows)
            copies.append(
                pltpu.make_async_copy(source.at[here], kept.at[here], sems.at[count[0]])
            )
            copies[-1].start()
            count[0] += 1
        return copies

    if first:
        ctx_copies = fetch(ctx_hbm, ctx, SEQ)
        depth_copies = fetch(depth_hbm, depth_in, SEQ)
    book_copies = [
        fetch(embed_hbm.at[book[0] + j], embed.at[j], 2)
        + fetch(heads_hbm.at[book[0] + j], heads.at[j], 4)
        for j in range(2)
    ]
    if first:
        total = None
        for part in range(SEQ):
            ctx_copies[part].wait()
            depth_copies[part].wait()
            term = jnp.dot(
                ctx[part],
                depth_in[part * PAIR : (part + 1) * PAIR],
                preferred_element_type=jnp.float32,
            )
            total = term if total is None else total + term
        projected[...] = total
    lane = lax.broadcasted_iota(jnp.int32, (FRAMES, CODEBOOKS), 1)
    both = []
    stores = []
    for j in range(2):
        c = book[0] + j
        for copy in book_copies[j]:
            copy.wait()
        token = jnp.sum(jnp.where(lane == c, target[...], 0), axis=1, keepdims=True)
        hidden, dlogits, loss = depth_head(
            projected[...], embed[j], gain[c], heads[j], bias[c], token
        )
        acts[0, j] = hidden
        acts[1, j] = dlogits
        both.append(loss)
        if first:
            for kind in range(2):
                copy = pltpu.make_async_copy(
                    acts.at[kind, j], acts_hbm.at[kind, j], sems.at[count[0]]
                )
                copy.start()
                stores.append(copy)
                count[0] += 1
    pair_lane = lax.broadcasted_iota(jnp.int32, (FRAMES, 2), 1)
    losses[...] = jnp.where(pair_lane == 0, both[0], both[1])
    for copy in stores:
        copy.wait()


def depth_call(first, outs, book, hbm_args, vmem_args):
    scratch = [
        pltpu.VMEM((2, FRAMES, DEPTH_DIM), jnp.bfloat16),
        pltpu.VMEM((2, DEPTH_DIM, VOCAB), jnp.bfloat16),
        pltpu.SemaphoreType.DMA((32 if first else 12,)),
    ]
    if first:
        scratch = [
            pltpu.VMEM((2, 2, FRAMES, DEPTH_DIM), jnp.bfloat16),
            pltpu.VMEM((SEQ, FRAMES, PAIR), jnp.bfloat16),
            pltpu.VMEM((FEATURES, DEPTH_DIM), jnp.bfloat16),
        ] + scratch
    in_specs = [HBM] * len(hbm_args) + [VMEM] * len(vmem_args)
    if not first:
        in_specs[0] = VMEM
    return pl.pallas_call(
        partial(depth_kernel, first),
        out_shape=outs,
        in_specs=[SMEM] + in_specs,
        out_specs=(VMEM, HBM, VMEM) if first else (VMEM, VMEM),
        scratch_shapes=scratch,
        compiler_params=pltpu.CompilerParams(vmem_limit_bytes=DEPTH_GRANT),
        cost_estimate=pl.CostEstimate(
            flops=2 * 2 * FRAMES * DEPTH_DIM * VOCAB,
            bytes_accessed=8 * 2**20,
            transcendentals=2 * FRAMES * VOCAB,
        ),
    )(book.reshape(1), *hbm_args, *vmem_args)


def outer_kernel(mine, theirs, out_hbm, out, sems):
    chunk = 128
    stores = []
    for step in range(DEPTH_DIM // chunk):
        at = step * chunk
        both = []
        for j in range(2):
            total = None
            for acts in (mine, theirs):
                term = lax.dot_general(
                    acts[0, j, :, at : at + chunk],
                    acts[1, j],
                    (((0,), (0,)), ((), ())),
                    preferred_element_type=jnp.float32,
                )
                total = term if total is None else total + term
            both.append(total.reshape(chunk // 8, 8, VOCAB))
        here = slice(at // 8, (at + chunk) // 8)
        out[here] = jnp.concatenate(both, axis=1).astype(jnp.bfloat16)
        copy = pltpu.make_async_copy(out.at[here], out_hbm.at[here], sems.at[step])
        copy.start()
        stores.append(copy)
    for copy in stores:
        copy.wait()


def outer(mine, theirs):
    return pl.pallas_call(
        outer_kernel,
        out_shape=pltpu.HBM((SEQ * WIDE, 16, VOCAB), jnp.bfloat16),
        in_specs=[VMEM] * 2,
        out_specs=HBM,
        scratch_shapes=[
            pltpu.VMEM((SEQ * WIDE, 16, VOCAB), jnp.bfloat16),
            pltpu.SemaphoreType.DMA((8,)),
        ],
        compiler_params=pltpu.CompilerParams(vmem_limit_bytes=40 * 2**20),
        cost_estimate=pl.CostEstimate(
            flops=2 * 2 * 2 * FRAMES * DEPTH_DIM * VOCAB,
            bytes_accessed=8 * 2**20,
            transcendentals=0,
        ),
    )(mine, theirs)


def total_kernel(scale, shares_hbm, out, shares, sems):
    chips = SEQ * WIDE // 2
    step = chips // 16
    loads = [
        pltpu.make_async_copy(
            shares_hbm.at[i * step : (i + 1) * step],
            shares.at[i * step : (i + 1) * step],
            sems.at[i],
        )
        for i in range(16)
    ]
    for copy in loads:
        copy.start()
    acc = None
    for i in range(16):
        loads[i].wait()
        term = jnp.sum(shares[i * step : (i + 1) * step].astype(jnp.float32), axis=0)
        acc = term if acc is None else acc + term
    for book in range(CODEBOOKS):
        out[:, book] = acc[book // 2, 8 * (book % 2) : 8 * (book % 2) + 8, :] * scale


def total(shares, scale):
    chips = SEQ * WIDE // 2
    return pl.pallas_call(
        partial(total_kernel, scale),
        out_shape=jax.ShapeDtypeStruct((8, CODEBOOKS, VOCAB), jnp.float32),
        in_specs=[HBM],
        out_specs=VMEM,
        scratch_shapes=[
            pltpu.VMEM((chips, 2, 16, VOCAB), jnp.bfloat16),
            pltpu.SemaphoreType.DMA((16,)),
        ],
        compiler_params=pltpu.CompilerParams(vmem_limit_bytes=GRANT),
        cost_estimate=pl.CostEstimate(
            flops=chips * 32 * VOCAB, bytes_accessed=chips * 64 * VOCAB, transcendentals=0
        ),
    )(shares.reshape(chips, 2, 16, VOCAB))


def normalize(norm_gain, mixed_in):
    return (
        mixed_in
        * lax.rsqrt(jnp.mean(mixed_in * mixed_in, axis=-1, keepdims=True) + 1e-05)
        * norm_gain[:, None, :]
    )


def swap_wide(array, stride):
    return lax.ppermute(array, "wide", [(i, i ^ stride) for i in range(WIDE)])


def share_out(rows):
    place = lax.axis_index("wide")
    held = rows.reshape(2, 2, 2, 2, rows.shape[1])
    for axis, stride in enumerate((8, 4, 2, 1)):
        high = (place // stride) % 2 == 1
        low_part = lax.index_in_dim(held, 0, axis, keepdims=True)
        high_part = lax.index_in_dim(held, 1, axis, keepdims=True)
        kept = jnp.where(high, high_part, low_part)
        came = swap_wide(jnp.where(high, low_part, high_part), stride)
        held = jnp.concatenate(
            (jnp.where(high, came, kept), jnp.where(high, kept, came)), axis=axis
        )
    return held.reshape(WIDE, rows.shape[1])


def shards(
    queries, key_vectors, values, audio_codes, depth_in, code_embed, norm_gain, out_heads, out_bias
):
    core = lax.axis_index("wide") % 2
    qkv = lax.all_to_all(pack(queries, key_vectors, values), "seq", 0, 0, tiled=True)
    targets = share_out(audio_codes.reshape(WIDE, 64)).reshape(FRAMES, CODEBOOKS)
    looked = lookup(targets, code_embed)
    heads = out_heads.transpose(1, 0, 2)
    qkv, looked, heads = lax.optimization_barrier((qkv, looked, heads))
    small = (norm_gain[:, None, :], out_bias[:, None, :], targets)

    context = lax.all_to_all(
        attend(qkv), "seq", 0, 0, tiled=True
    )
    mine = 2 * core
    other = 2 - mine
    acts_shape = jax.ShapeDtypeStruct((2, 2, FRAMES, DEPTH_DIM), jnp.bfloat16)
    losses_shape = jax.ShapeDtypeStruct((FRAMES, 2), jnp.float32)
    projected, acts_other, losses_other = depth_call(
        True,
        (
            jax.ShapeDtypeStruct((FRAMES, DEPTH_DIM), jnp.float32),
            pltpu.HBM(acts_shape.shape, acts_shape.dtype),
            losses_shape,
        ),
        other,
        (context, depth_in, looked, heads),
        small,
    )
    came = swap_wide(acts_other, 1)
    acts_mine, losses_mine = depth_call(
        False, (acts_shape, losses_shape), mine, (projected, looked, heads), small
    )
    shares = lax.all_to_all(outer(acts_mine, came), ("seq", "wide"), 0, 0, tiled=True)
    grad_scale = (VOCAB / (SEQ * WIDE * FRAMES)) ** 0.5
    head_grads = total(shares, grad_scale)

    def in_order(of_mine, of_other):
        low = jnp.where(core == 0, of_mine, of_other)
        high = jnp.where(core == 0, of_other, of_mine)
        return jnp.concatenate((low, high), axis=0)

    dlogits = in_order(acts_mine[1], acts_other[1])
    pullback = jax.vjp(
        partial(normalize, norm_gain), projected[None] + looked.astype(jnp.float32)
    )[1]
    dhidden = jnp.einsum("cnv,cev->cne", dlogits, heads, preferred_element_type=jnp.float32)
    dmixed = pullback(dhidden)[0]
    dprojected = jnp.sum(dmixed, axis=0).astype(jnp.bfloat16)
    context_grad = lax.dot_general(
        dprojected, depth_in, (((1,), (1,)), ((), ())), preferred_element_type=jnp.float32
    ).astype(jnp.bfloat16)
    losses = jnp.where(
        core == 0,
        jnp.concatenate((losses_mine, losses_other), axis=1),
        jnp.concatenate((losses_other, losses_mine), axis=1),
    )
    losses, context_grad = lax.optimization_barrier((losses, context_grad))
    frame_losses = share_out(losses.reshape(WIDE, 64)).reshape(WIDE, 16, CODEBOOKS)
    return (frame_losses, context_grad.reshape(1, FRAMES, FEATURES), head_grads)


def solution(mesh):
    return jax.shard_map(
        shards,
        mesh=mesh,
        in_specs=(
            P("wide", "seq", None),
            P("wide", "seq", None),
            P("wide", "seq", None),
            P(None, ("seq", "wide"), None),
            P(),
            P(),
            P(),
            P(),
            P(),
        ),
        out_specs=(
            P(None, ("seq", "wide"), None),
            P("wide", "seq", None),
            P(("seq", "wide"), None, None),
        ),
        check_vma=False,
    )
```

```python
from functools import partial

import jax
import jax.numpy as jnp
from jax import lax
from jax.experimental import pallas as pl
from jax.experimental.pallas import tpu as pltpu
from jax.sharding import PartitionSpec as P

HEADS = 16
HEAD_DIM = 128
FEATURES = 2048
DEPTH_DIM = 1024
CODEBOOKS = 4
VOCAB = 1024
SEQ = 8
WIDE = 16
FRAMES = 256
LENGTH = SEQ * FRAMES
PAIR = 2 * HEAD_DIM


def attend_kernel(qkv, out_hbm, out, out_sems):
    stores = [
        pltpu.make_async_copy(out.at[i], out_hbm.at[i], out_sems.at[i]) for i in range(SEQ)
    ]
    to_exp2 = HEAD_DIM ** (-0.5) * 1.4426950408889634
    row = lax.broadcasted_iota(jnp.int32, (FRAMES, FRAMES), 0)
    col = lax.broadcasted_iota(jnp.int32, (FRAMES, FRAMES), 1)
    across = (((1,), (1,)), ((), ()))
    for block in range(SEQ):
        for head in range(2):
            at = head * HEAD_DIM
            q = qkv[block, :, at : at + HEAD_DIM]
            diag = lax.dot_general(
                q,
                qkv[block, :, PAIR + at : PAIR + at + HEAD_DIM],
                across,
                preferred_element_type=jnp.float32,
            )
            diag = jnp.where(col <= row, diag, -jnp.inf)
            top = jnp.max(diag, axis=1, keepdims=True)
            if block:
                keys = qkv[:block, :, PAIR + at : PAIR + at + HEAD_DIM]
                past = lax.dot_general(
                    q,
                    keys.reshape(block * FRAMES, HEAD_DIM),
                    across,
                    preferred_element_type=jnp.float32,
                )
                top = jnp.maximum(top, jnp.max(past, axis=1, keepdims=True))
            weights = jnp.exp2((diag - top) * to_exp2)
            total = jnp.sum(weights, axis=1, keepdims=True)
            acc = jnp.dot(
                weights.astype(jnp.bfloat16),
                qkv[block, :, 2 * PAIR + at : 2 * PAIR + at + HEAD_DIM],
                preferred_element_type=jnp.float32,
            )
            if block:
                weights = jnp.exp2((past - top) * to_exp2)
                total = total + jnp.sum(weights, axis=1, keepdims=True)
                vals = qkv[:block, :, 2 * PAIR + at : 2 * PAIR + at + HEAD_DIM]
                acc = acc + jnp.dot(
                    weights.astype(jnp.bfloat16),
                    vals.reshape(block * FRAMES, HEAD_DIM),
                    preferred_element_type=jnp.float32,
                )
            out[block, :, at : at + HEAD_DIM] = (acc / total).astype(jnp.bfloat16)
        stores[block].start()
    for copy in stores:
        copy.wait()


HBM = pl.BlockSpec(memory_space=pltpu.HBM)
VMEM = pl.BlockSpec(memory_space=pltpu.VMEM)
SMEM = pl.BlockSpec(memory_space=pltpu.SMEM)
GRANT = 60 * 2**20
DEPTH_GRANT = 44 * 2**20


def attend(qkv):
    return pl.pallas_call(
        attend_kernel,
        out_shape=pltpu.HBM((SEQ, FRAMES, PAIR), jnp.bfloat16),
        in_specs=[VMEM],
        out_specs=HBM,
        scratch_shapes=[
            pltpu.VMEM((SEQ, FRAMES, PAIR), jnp.bfloat16),
            pltpu.SemaphoreType.DMA((SEQ,)),
        ],
        compiler_params=pltpu.CompilerParams(vmem_limit_bytes=40 * 2**20),
        cost_estimate=pl.CostEstimate(
            flops=2 * 36 * FRAMES * FRAMES * HEAD_DIM * 4,
            bytes_accessed=LENGTH * PAIR * 8,
            transcendentals=2 * 36 * FRAMES * FRAMES,
        ),
    )(qkv)


def pack_kernel(queries, key_vectors, values, out, held, in_sems, out_sems):
    rows = FRAMES // 4
    sources = (queries, key_vectors, values)
    loads = [
        [
            pltpu.make_async_copy(
                ref.at[0, i * rows : (i + 1) * rows],
                held.at[kind, i * rows : (i + 1) * rows],
                in_sems.at[i, kind],
            )
            for kind, ref in enumerate(sources)
        ]
        for i in range(4)
    ]
    for group in loads:
        for copy in group:
            copy.start()
    stores = []
    for i in range(4):
        for kind in range(3):
            loads[i][kind].wait()
            for part in range(SEQ):
                copy = pltpu.make_async_copy(
                    held.at[kind, i * rows : (i + 1) * rows, part * PAIR : (part + 1) * PAIR],
                    out.at[part, i * rows : (i + 1) * rows, kind * PAIR : (kind + 1) * PAIR],
                    out_sems.at[i, kind, part],
                )
                copy.start()
                stores.append(copy)
    for copy in stores:
        copy.wait()


def pack(queries, key_vectors, values):
    return pl.pallas_call(
        pack_kernel,
        out_shape=pltpu.HBM((SEQ, FRAMES, 3 * PAIR), jnp.bfloat16),
        in_specs=[HBM] * 3,
        out_specs=HBM,
        scratch_shapes=[
            pltpu.VMEM((3, FRAMES, FEATURES), jnp.bfloat16),
            pltpu.SemaphoreType.DMA((4, 3)),
            pltpu.SemaphoreType.DMA((4, 3, SEQ)),
        ],
        compiler_params=pltpu.CompilerParams(vmem_limit_bytes=GRANT),
        cost_estimate=pl.CostEstimate(flops=0, bytes_accessed=6 * 2**20, transcendentals=0),
    )(queries, key_vectors, values)


def lookup_kernel(target, table_hbm, looked_hbm, table, out, in_sems, out_sems):
    books = CODEBOOKS - 1
    loads = [
        pltpu.make_async_copy(table_hbm.at[c], table.at[c], in_sems.at[c]) for c in range(books)
    ]
    stores = [
        pltpu.make_async_copy(out.at[c], looked_hbm.at[c], out_sems.at[c])
        for c in range(CODEBOOKS)
    ]
    for copy in loads:
        copy.start()
    out[0] = jnp.zeros((FRAMES, DEPTH_DIM), jnp.bfloat16)
    stores[0].start()
    for c in range(books):
        loads[c].wait()
        chosen = lax.broadcasted_iota(jnp.int32, (FRAMES, VOCAB), 1) == target[:, c : c + 1]
        out[c + 1] = jnp.dot(
            chosen.astype(jnp.float32).astype(jnp.bfloat16),
            table[c],
            preferred_element_type=jnp.float32,
        ).astype(jnp.bfloat16)
        stores[c + 1].start()
    for copy in stores:
        copy.wait()


def lookup(target, table):
    return pl.pallas_call(
        lookup_kernel,
        out_shape=pltpu.HBM((CODEBOOKS, FRAMES, DEPTH_DIM), jnp.bfloat16),
        in_specs=[VMEM, HBM],
        out_specs=HBM,
        scratch_shapes=[
            pltpu.VMEM((CODEBOOKS - 1, VOCAB, DEPTH_DIM), jnp.bfloat16),
            pltpu.VMEM((CODEBOOKS, FRAMES, DEPTH_DIM), jnp.bfloat16),
            pltpu.SemaphoreType.DMA((CODEBOOKS - 1,)),
            pltpu.SemaphoreType.DMA((CODEBOOKS,)),
        ],
        compiler_params=pltpu.CompilerParams(vmem_limit_bytes=GRANT),
        cost_estimate=pl.CostEstimate(
            flops=6 * FRAMES * VOCAB * DEPTH_DIM, bytes_accessed=10 * 2**20, transcendentals=0
        ),
    )(target, table)


def depth_head(projected, embed, gain, heads, bias, target):
    mixed = projected + embed.astype(jnp.float32)
    scale = lax.rsqrt(jnp.mean(mixed * mixed, axis=1, keepdims=True) + 1e-05)
    hidden = (mixed * scale * gain).astype(jnp.bfloat16)
    logits = jnp.dot(hidden, heads, preferred_element_type=jnp.float32) + bias
    top = jnp.max(logits, axis=1, keepdims=True)
    shifted = jnp.exp(logits - top)
    total = jnp.sum(shifted, axis=1, keepdims=True)
    onehot = lax.broadcasted_iota(jnp.int32, (FRAMES, VOCAB), 1) == target
    picked = jnp.sum(jnp.where(onehot, logits, 0.0), axis=1, keepdims=True)
    losses = top + jnp.log(total) - picked
    dlogits = (shifted / total - onehot.astype(jnp.float32)).astype(jnp.bfloat16)
    return hidden, dlogits, losses


def depth_pair(
    book, projected, embed, heads, gain, bias, target, acts, losses, begin=None, finish=None
):
    lane = lax.broadcasted_iota(jnp.int32, (FRAMES, CODEBOOKS), 1)
    both = []
    for j in range(2):
        c = book[0] + j
        if begin:
            begin(j)
        token = jnp.sum(jnp.where(lane == c, target[...], 0), axis=1, keepdims=True)
        hidden, dlogits, loss = depth_head(
            projected[...], embed[j], gain[c], heads[j], bias[c], token
        )
        acts[0, j] = hidden
        acts[1, j] = dlogits
        if finish:
            finish(j)
        both.append(loss)
    pair_lane = lax.broadcasted_iota(jnp.int32, (FRAMES, 2), 1)
    losses[...] = jnp.where(pair_lane == 0, both[0], both[1])


def first_kernel(
    book,
    ctx,
    gain,
    bias,
    target,
    depth_hbm,
    looked_hbm,
    heads_hbm,
    projected,
    acts_hbm,
    losses,
    next_embed,
    next_heads,
    acts,
    depth_in,
    embed,
    heads,
    depth_sems,
    book_sems,
    next_sems,
    out_sems,
):
    rows = [slice(part * PAIR, (part + 1) * PAIR) for part in range(SEQ)]
    depth_copies = [
        pltpu.make_async_copy(depth_hbm.at[rows[part]], depth_in.at[rows[part]], depth_sems.at[part])
        for part in range(SEQ)
    ]
    book_copies = [
        [
            pltpu.make_async_copy(looked_hbm.at[book[0] + j], embed.at[j], book_sems.at[0, j]),
            pltpu.make_async_copy(heads_hbm.at[book[0] + j], heads.at[j], book_sems.at[1, j]),
        ]
        for j in range(2)
    ]
    staged = []
    for j in range(2):
        c = book[1] + j
        staged.append(
            pltpu.make_async_copy(looked_hbm.at[c], next_embed.at[j], next_sems.at[0, j])
        )
        staged.append(
            pltpu.make_async_copy(heads_hbm.at[c], next_heads.at[j], next_sems.at[1, j])
        )
    for copy in depth_copies + book_copies[0] + book_copies[1] + staged:
        copy.start()
    total = None
    for part in range(SEQ):
        depth_copies[part].wait()
        term = jnp.dot(ctx[part], depth_in[rows[part]], preferred_element_type=jnp.float32)
        total = term if total is None else total + term
    projected[...] = total
    stores = [
        [
            pltpu.make_async_copy(acts.at[kind, j], acts_hbm.at[kind, j], out_sems.at[kind, j])
            for kind in range(2)
        ]
        for j in range(2)
    ]

    def begin(j):
        for copy in book_copies[j]:
            copy.wait()

    def finish(j):
        for copy in stores[j]:
            copy.start()

    depth_pair(book, projected, embed, heads, gain, bias, target, acts, losses, begin, finish)
    for copy in staged + stores[0] + stores[1]:
        copy.wait()


def second_kernel(book, projected, embed, heads, gain, bias, target, acts, losses):
    depth_pair(book, projected, embed, heads, gain, bias, target, acts, losses)


DEPTH_COST = pl.CostEstimate(
    flops=2 * 2 * FRAMES * DEPTH_DIM * VOCAB,
    bytes_accessed=8 * 2**20,
    transcendentals=2 * FRAMES * VOCAB,
)
ACTS = (2, 2, FRAMES, DEPTH_DIM)


def depth_first(books, context, small, depth_in, looked, heads):
    return pl.pallas_call(
        first_kernel,
        out_shape=(
            jax.ShapeDtypeStruct((FRAMES, DEPTH_DIM), jnp.float32),
            pltpu.HBM(ACTS, jnp.bfloat16),
            jax.ShapeDtypeStruct((FRAMES, 2), jnp.float32),
            pltpu.VMEM((2, FRAMES, DEPTH_DIM), jnp.bfloat16),
            pltpu.VMEM((2, DEPTH_DIM, VOCAB), jnp.bfloat16),
        ),
        in_specs=[SMEM] + [VMEM] * 4 + [HBM] * 3,
        out_specs=(VMEM, HBM, VMEM, VMEM, VMEM),
        scratch_shapes=[
            pltpu.VMEM(ACTS, jnp.bfloat16),
            pltpu.VMEM((FEATURES, DEPTH_DIM), jnp.bfloat16),
            pltpu.VMEM((2, FRAMES, DEPTH_DIM), jnp.bfloat16),
            pltpu.VMEM((2, DEPTH_DIM, VOCAB), jnp.bfloat16),
            pltpu.SemaphoreType.DMA((SEQ,)),
            pltpu.SemaphoreType.DMA((2, 2)),
            pltpu.SemaphoreType.DMA((2, 2)),
            pltpu.SemaphoreType.DMA((2, 2)),
        ],
        compiler_params=pltpu.CompilerParams(vmem_limit_bytes=DEPTH_GRANT),
        cost_estimate=DEPTH_COST,
    )(books, context, *small, depth_in, looked, heads)


def depth_second(book, projected, embed, heads, small):
    return pl.pallas_call(
        second_kernel,
        out_shape=(
            jax.ShapeDtypeStruct(ACTS, jnp.bfloat16),
            jax.ShapeDtypeStruct((FRAMES, 2), jnp.float32),
        ),
        in_specs=[SMEM] + [VMEM] * 6,
        out_specs=(VMEM, VMEM),
        compiler_params=pltpu.CompilerParams(vmem_limit_bytes=DEPTH_GRANT),
        cost_estimate=DEPTH_COST,
    )(book.reshape(1), projected, embed, heads, *small)


def outer_kernel(mine, theirs, out_hbm, out, sems):
    chunk = 128
    stores = []
    for step in range(DEPTH_DIM // chunk):
        at = step * chunk
        both = []
        for j in range(2):
            total = None
            for acts in (mine, theirs):
                term = lax.dot_general(
                    acts[0, j, :, at : at + chunk],
                    acts[1, j],
                    (((0,), (0,)), ((), ())),
                    preferred_element_type=jnp.float32,
                )
                total = term if total is None else total + term
            both.append(total.reshape(chunk // 8, 8, VOCAB))
        here = slice(at // 8, (at + chunk) // 8)
        out[here] = jnp.concatenate(both, axis=1).astype(jnp.bfloat16)
        copy = pltpu.make_async_copy(out.at[here], out_hbm.at[here], sems.at[step])
        copy.start()
        stores.append(copy)
    for copy in stores:
        copy.wait()


def outer(mine, theirs):
    return pl.pallas_call(
        outer_kernel,
        out_shape=pltpu.HBM((SEQ * WIDE, 16, VOCAB), jnp.bfloat16),
        in_specs=[VMEM] * 2,
        out_specs=HBM,
        scratch_shapes=[
            pltpu.VMEM((SEQ * WIDE, 16, VOCAB), jnp.bfloat16),
            pltpu.SemaphoreType.DMA((8,)),
        ],
        compiler_params=pltpu.CompilerParams(vmem_limit_bytes=40 * 2**20),
        cost_estimate=pl.CostEstimate(
            flops=2 * 2 * 2 * FRAMES * DEPTH_DIM * VOCAB,
            bytes_accessed=8 * 2**20,
            transcendentals=0,
        ),
    )(mine, theirs)


def total_kernel(scale, shares_hbm, out, shares, sems):
    chips = SEQ * WIDE // 2
    step = chips // 16
    loads = [
        pltpu.make_async_copy(
            shares_hbm.at[i * step : (i + 1) * step],
            shares.at[i * step : (i + 1) * step],
            sems.at[i],
        )
        for i in range(16)
    ]
    for copy in loads:
        copy.start()
    acc = None
    for i in range(16):
        loads[i].wait()
        term = jnp.sum(shares[i * step : (i + 1) * step].astype(jnp.float32), axis=0)
        acc = term if acc is None else acc + term
    for book in range(CODEBOOKS):
        out[:, book] = acc[book // 2, 8 * (book % 2) : 8 * (book % 2) + 8, :] * scale


def total(shares, scale):
    chips = SEQ * WIDE // 2
    return pl.pallas_call(
        partial(total_kernel, scale),
        out_shape=jax.ShapeDtypeStruct((8, CODEBOOKS, VOCAB), jnp.float32),
        in_specs=[HBM],
        out_specs=VMEM,
        scratch_shapes=[
            pltpu.VMEM((chips, 2, 16, VOCAB), jnp.bfloat16),
            pltpu.SemaphoreType.DMA((16,)),
        ],
        compiler_params=pltpu.CompilerParams(vmem_limit_bytes=GRANT),
        cost_estimate=pl.CostEstimate(
            flops=chips * 32 * VOCAB, bytes_accessed=chips * 64 * VOCAB, transcendentals=0
        ),
    )(shares.reshape(chips, 2, 16, VOCAB))


def normalize(norm_gain, mixed_in):
    return (
        mixed_in
        * lax.rsqrt(jnp.mean(mixed_in * mixed_in, axis=-1, keepdims=True) + 1e-05)
        * norm_gain[:, None, :]
    )


def swap_wide(array, stride):
    return lax.ppermute(array, "wide", [(i, i ^ stride) for i in range(WIDE)])


def share_step(held, axis, stride):
    high = (lax.axis_index("wide") // stride) % 2 == 1
    low_part = lax.index_in_dim(held, 0, axis, keepdims=True)
    high_part = lax.index_in_dim(held, 1, axis, keepdims=True)
    kept = jnp.where(high, high_part, low_part)
    came = swap_wide(jnp.where(high, low_part, high_part), stride)
    return jnp.concatenate(
        (jnp.where(high, came, kept), jnp.where(high, kept, came)), axis=axis
    )


def by_distance(rows):
    index = jnp.arange(WIDE, dtype=jnp.int32)
    pick = index[:, None] == (index[None, :] ^ lax.axis_index("wide"))
    return jnp.sum(jnp.where(pick[:, :, None], rows[None], 0), axis=1)


def share_out(rows):
    sent = by_distance(rows).reshape(4, 4, rows.shape[1])
    first = jnp.stack([sent[0]] + [swap_wide(sent[k], 4 * k) for k in range(1, 4)])
    second = [first[:, 0]] + [swap_wide(first[:, k], k) for k in range(1, 4)]
    return by_distance(jnp.stack(second, axis=1).reshape(WIDE, rows.shape[1]))


def shards(
    queries, key_vectors, values, audio_codes, depth_in, code_embed, norm_gain, out_heads, out_bias
):
    core = lax.axis_index("wide") % 2
    packed = pack(queries, key_vectors, values)
    held, packed = lax.optimization_barrier((audio_codes, packed))
    held = share_step(held.reshape(2, 2, 2, 2, 64), 0, 8)
    held = share_step(held, 1, 4)
    qkv = lax.all_to_all(packed, "seq", 0, 0, tiled=True)
    heads = out_heads.transpose(1, 0, 2)
    held, qkv, heads = lax.optimization_barrier((held, qkv, heads))
    held = share_step(held, 2, 2)
    context = attend(qkv)
    held, context = lax.optimization_barrier((held, context))
    context = lax.all_to_all(context, "seq", 0, 0, tiled=True)
    held = share_step(held, 3, 1)
    targets = held.reshape(FRAMES, CODEBOOKS)
    small = (norm_gain[:, None, :], out_bias[:, None, :], targets)
    mine = 2 * core
    other = 2 - mine
    looked = lookup(targets, code_embed)
    projected, acts_other, losses_other, *staged = depth_first(
        jnp.stack([other, mine]), context, small, depth_in, pltpu.with_memory_space_constraint(looked, pltpu.HBM), heads
    )
    came = swap_wide(acts_other, 1)
    acts_mine, losses_mine = depth_second(mine, projected, *staged, small)
    shares = lax.all_to_all(outer(acts_mine, came), ("seq", "wide"), 0, 0, tiled=True)
    grad_scale = (VOCAB / (SEQ * WIDE * FRAMES)) ** 0.5
    head_grads = total(shares, grad_scale)

    def in_order(of_mine, of_other):
        low = jnp.where(core == 0, of_mine, of_other)
        high = jnp.where(core == 0, of_other, of_mine)
        return jnp.concatenate((low, high), axis=0)

    dlogits = in_order(acts_mine[1], acts_other[1])
    pullback = jax.vjp(
        partial(normalize, norm_gain), projected[None] + looked.astype(jnp.float32)
    )[1]
    dhidden = jnp.einsum("cnv,cev->cne", dlogits, heads, preferred_element_type=jnp.float32)
    dmixed = pullback(dhidden)[0]
    dprojected = jnp.sum(dmixed, axis=0).astype(jnp.bfloat16)
    context_grad = lax.dot_general(
        dprojected, depth_in, (((1,), (1,)), ((), ())), preferred_element_type=jnp.float32
    ).astype(jnp.bfloat16)
    losses = jnp.where(
        core == 0,
        jnp.concatenate((losses_mine, losses_other), axis=1),
        jnp.concatenate((losses_other, losses_mine), axis=1),
    )
    losses, context_grad = lax.optimization_barrier((losses, context_grad))
    frame_losses = share_out(losses.reshape(WIDE, 64)).reshape(WIDE, 16, CODEBOOKS)
    return (frame_losses, context_grad.reshape(1, FRAMES, FEATURES), head_grads)


def solution(mesh):
    return jax.shard_map(
        shards,
        mesh=mesh,
        in_specs=(
            P("wide", "seq", None),
            P("wide", "seq", None),
            P("wide", "seq", None),
            P(None, ("seq", "wide"), None),
            P(),
            P(),
            P(),
            P(),
            P(),
        ),
        out_specs=(
            P(None, ("seq", "wide"), None),
            P("wide", "seq", None),
            P(("seq", "wide"), None, None),
        ),
        check_vma=False,
    )
```

```python
from functools import partial

import jax
import jax.numpy as jnp
from jax import lax
from jax.experimental import pallas as pl
from jax.experimental.pallas import tpu as pltpu
from jax.sharding import PartitionSpec as P

HEADS = 16
HEAD_DIM = 128
FEATURES = 2048
DEPTH_DIM = 1024
CODEBOOKS = 4
VOCAB = 1024
SEQ = 8
WIDE = 16
FRAMES = 256
LENGTH = SEQ * FRAMES
PAIR = 2 * HEAD_DIM


def attend_kernel(qkv, out_hbm, out, out_sems):
    stores = [
        pltpu.make_async_copy(out.at[i], out_hbm.at[i], out_sems.at[i]) for i in range(SEQ)
    ]
    to_exp2 = HEAD_DIM ** (-0.5) * 1.4426950408889634
    row = lax.broadcasted_iota(jnp.int32, (FRAMES, FRAMES), 0)
    col = lax.broadcasted_iota(jnp.int32, (FRAMES, FRAMES), 1)
    across = (((1,), (1,)), ((), ()))
    ones = jnp.ones((LENGTH, HEAD_DIM), jnp.bfloat16)

    def scores(block, head):
        at = head * HEAD_DIM
        q = qkv[block, :, at : at + HEAD_DIM]
        diag = lax.dot_general(
            q,
            qkv[block, :, PAIR + at : PAIR + at + HEAD_DIM],
            across,
            preferred_element_type=jnp.float32,
        )
        if not block:
            return (diag,)
        keys = qkv[:block, :, PAIR + at : PAIR + at + HEAD_DIM]
        past = lax.dot_general(
            q,
            keys.reshape(block * FRAMES, HEAD_DIM),
            across,
            preferred_element_type=jnp.float32,
        )
        return (diag, past)

    def combine(block, head, parts):
        at = 2 * PAIR + head * HEAD_DIM
        parts = (jnp.where(col <= row, parts[0], -jnp.inf),) + parts[1:]
        tops = [jnp.max(part, axis=1, keepdims=True) for part in parts]
        top = tops[0] if not block else jnp.maximum(*tops)
        acc = None
        for part, first, last in zip(parts, (block, 0), (block + 1, block)):
            weights = jnp.exp2((part - top) * to_exp2).astype(jnp.bfloat16)
            vals = qkv[first:last, :, at : at + HEAD_DIM].reshape(-1, HEAD_DIM)
            vals = jnp.concatenate((vals, ones[: vals.shape[0]]), axis=1)
            term = jnp.dot(weights, vals, preferred_element_type=jnp.float32)
            acc = term if acc is None else acc + term
        out[block, :, head * HEAD_DIM : (head + 1) * HEAD_DIM] = (
            acc[:, :HEAD_DIM] / acc[:, HEAD_DIM:]
        ).astype(jnp.bfloat16)

    tasks = [(block, head) for block in range(SEQ) for head in range(2)]
    present = scores(*tasks[0])
    for i, (block, head) in enumerate(tasks):
        following = scores(*tasks[i + 1]) if i + 1 < len(tasks) else None
        combine(block, head, present)
        present = following
        if head == 1:
            stores[block].start()
    for copy in stores:
        copy.wait()


HBM = pl.BlockSpec(memory_space=pltpu.HBM)
VMEM = pl.BlockSpec(memory_space=pltpu.VMEM)
SMEM = pl.BlockSpec(memory_space=pltpu.SMEM)
GRANT = 60 * 2**20
DEPTH_GRANT = 44 * 2**20


def attend(qkv):
    return pl.pallas_call(
        attend_kernel,
        out_shape=pltpu.HBM((SEQ, FRAMES, PAIR), jnp.bfloat16),
        in_specs=[VMEM],
        out_specs=HBM,
        scratch_shapes=[
            pltpu.VMEM((SEQ, FRAMES, PAIR), jnp.bfloat16),
            pltpu.SemaphoreType.DMA((SEQ,)),
        ],
        compiler_params=pltpu.CompilerParams(vmem_limit_bytes=40 * 2**20),
        cost_estimate=pl.CostEstimate(
            flops=2 * 36 * FRAMES * FRAMES * HEAD_DIM * 4,
            bytes_accessed=LENGTH * PAIR * 8,
            transcendentals=2 * 36 * FRAMES * FRAMES,
        ),
    )(qkv)


def pack_kernel(queries, key_vectors, values, out, held, in_sems, out_sems):
    rows = FRAMES // 4
    sources = (queries, key_vectors, values)
    loads = [
        [
            pltpu.make_async_copy(
                ref.at[0, i * rows : (i + 1) * rows],
                held.at[kind, i * rows : (i + 1) * rows],
                in_sems.at[i, kind],
            )
            for kind, ref in enumerate(sources)
        ]
        for i in range(4)
    ]
    for group in loads:
        for copy in group:
            copy.start()
    stores = []
    for i in range(4):
        for kind in range(3):
            loads[i][kind].wait()
            for part in range(SEQ):
                copy = pltpu.make_async_copy(
                    held.at[kind, i * rows : (i + 1) * rows, part * PAIR : (part + 1) * PAIR],
                    out.at[part, i * rows : (i + 1) * rows, kind * PAIR : (kind + 1) * PAIR],
                    out_sems.at[i, kind, part],
                )
                copy.start()
                stores.append(copy)
    for copy in stores:
        copy.wait()


def pack(queries, key_vectors, values):
    return pl.pallas_call(
        pack_kernel,
        out_shape=pltpu.HBM((SEQ, FRAMES, 3 * PAIR), jnp.bfloat16),
        in_specs=[HBM] * 3,
        out_specs=HBM,
        scratch_shapes=[
            pltpu.VMEM((3, FRAMES, FEATURES), jnp.bfloat16),
            pltpu.SemaphoreType.DMA((4, 3)),
            pltpu.SemaphoreType.DMA((4, 3, SEQ)),
        ],
        compiler_params=pltpu.CompilerParams(vmem_limit_bytes=GRANT),
        cost_estimate=pl.CostEstimate(flops=0, bytes_accessed=6 * 2**20, transcendentals=0),
    )(queries, key_vectors, values)


def lookup_kernel(target, table_hbm, looked_hbm, table, out, in_sems, out_sems):
    books = CODEBOOKS - 1
    loads = [
        pltpu.make_async_copy(table_hbm.at[c], table.at[c], in_sems.at[c]) for c in range(books)
    ]
    stores = [
        pltpu.make_async_copy(out.at[c], looked_hbm.at[c], out_sems.at[c])
        for c in range(CODEBOOKS)
    ]
    for copy in loads:
        copy.start()
    out[0] = jnp.zeros((FRAMES, DEPTH_DIM), jnp.bfloat16)
    stores[0].start()
    for c in range(books):
        loads[c].wait()
        chosen = lax.broadcasted_iota(jnp.int32, (FRAMES, VOCAB), 1) == target[:, c : c + 1]
        out[c + 1] = jnp.dot(
            chosen.astype(jnp.float32).astype(jnp.bfloat16),
            table[c],
            preferred_element_type=jnp.float32,
        ).astype(jnp.bfloat16)
        stores[c + 1].start()
    for copy in stores:
        copy.wait()


def lookup(target, table):
    return pl.pallas_call(
        lookup_kernel,
        out_shape=pltpu.HBM((CODEBOOKS, FRAMES, DEPTH_DIM), jnp.bfloat16),
        in_specs=[VMEM, HBM],
        out_specs=HBM,
        scratch_shapes=[
            pltpu.VMEM((CODEBOOKS - 1, VOCAB, DEPTH_DIM), jnp.bfloat16),
            pltpu.VMEM((CODEBOOKS, FRAMES, DEPTH_DIM), jnp.bfloat16),
            pltpu.SemaphoreType.DMA((CODEBOOKS - 1,)),
            pltpu.SemaphoreType.DMA((CODEBOOKS,)),
        ],
        compiler_params=pltpu.CompilerParams(vmem_limit_bytes=GRANT),
        cost_estimate=pl.CostEstimate(
            flops=6 * FRAMES * VOCAB * DEPTH_DIM, bytes_accessed=10 * 2**20, transcendentals=0
        ),
    )(target, table)


def depth_head(projected, embed, gain, heads, bias, target):
    mixed = projected + embed.astype(jnp.float32)
    scale = lax.rsqrt(jnp.mean(mixed * mixed, axis=1, keepdims=True) + 1e-05)
    hidden = (mixed * scale * gain).astype(jnp.bfloat16)
    logits = jnp.dot(hidden, heads, preferred_element_type=jnp.float32) + bias
    top = jnp.max(logits, axis=1, keepdims=True)
    shifted = jnp.exp(logits - top)
    total = jnp.sum(shifted, axis=1, keepdims=True)
    onehot = lax.broadcasted_iota(jnp.int32, (FRAMES, VOCAB), 1) == target
    picked = jnp.sum(jnp.where(onehot, logits, 0.0), axis=1, keepdims=True)
    losses = top + jnp.log(total) - picked
    dlogits = (shifted / total - onehot.astype(jnp.float32)).astype(jnp.bfloat16)
    return hidden, dlogits, losses


def depth_pair(
    book, projected, embed, heads, gain, bias, target, acts, losses, begin=None, finish=None
):
    lane = lax.broadcasted_iota(jnp.int32, (FRAMES, CODEBOOKS), 1)
    both = []
    for j in range(2):
        c = book[0] + j
        if begin:
            begin(j)
        token = jnp.sum(jnp.where(lane == c, target[...], 0), axis=1, keepdims=True)
        hidden, dlogits, loss = depth_head(
            projected[...], embed[j], gain[c], heads[j], bias[c], token
        )
        acts[0, j] = hidden
        acts[1, j] = dlogits
        if finish:
            finish(j)
        both.append(loss)
    pair_lane = lax.broadcasted_iota(jnp.int32, (FRAMES, 2), 1)
    losses[...] = jnp.where(pair_lane == 0, both[0], both[1])


def first_kernel(
    book,
    ctx,
    gain,
    bias,
    target,
    depth_hbm,
    looked_hbm,
    heads_hbm,
    projected,
    acts_hbm,
    losses,
    next_embed,
    next_heads,
    acts,
    depth_in,
    embed,
    heads,
    depth_sems,
    book_sems,
    next_sems,
    out_sems,
):
    rows = [slice(part * PAIR, (part + 1) * PAIR) for part in range(SEQ)]
    depth_copies = [
        pltpu.make_async_copy(depth_hbm.at[rows[part]], depth_in.at[rows[part]], depth_sems.at[part])
        for part in range(SEQ)
    ]
    book_copies = [
        [
            pltpu.make_async_copy(looked_hbm.at[book[0] + j], embed.at[j], book_sems.at[0, j]),
            pltpu.make_async_copy(heads_hbm.at[book[0] + j], heads.at[j], book_sems.at[1, j]),
        ]
        for j in range(2)
    ]
    staged = []
    for j in range(2):
        c = book[1] + j
        staged.append(
            pltpu.make_async_copy(looked_hbm.at[c], next_embed.at[j], next_sems.at[0, j])
        )
        staged.append(
            pltpu.make_async_copy(heads_hbm.at[c], next_heads.at[j], next_sems.at[1, j])
        )
    for copy in depth_copies + book_copies[0] + book_copies[1] + staged:
        copy.start()
    total = None
    for part in range(SEQ):
        depth_copies[part].wait()
        term = jnp.dot(ctx[part], depth_in[rows[part]], preferred_element_type=jnp.float32)
        total = term if total is None else total + term
    projected[...] = total
    stores = [
        [
            pltpu.make_async_copy(acts.at[kind, j], acts_hbm.at[kind, j], out_sems.at[kind, j])
            for kind in range(2)
        ]
        for j in range(2)
    ]

    def begin(j):
        for copy in book_copies[j]:
            copy.wait()

    def finish(j):
        for copy in stores[j]:
            copy.start()

    depth_pair(book, projected, embed, heads, gain, bias, target, acts, losses, begin, finish)
    for copy in staged + stores[0] + stores[1]:
        copy.wait()


def second_kernel(book, projected, embed, heads, gain, bias, target, acts, losses):
    depth_pair(book, projected, embed, heads, gain, bias, target, acts, losses)


DEPTH_COST = pl.CostEstimate(
    flops=2 * 2 * FRAMES * DEPTH_DIM * VOCAB,
    bytes_accessed=8 * 2**20,
    transcendentals=2 * FRAMES * VOCAB,
)
ACTS = (2, 2, FRAMES, DEPTH_DIM)


def depth_first(books, context, small, depth_in, looked, heads):
    return pl.pallas_call(
        first_kernel,
        out_shape=(
            jax.ShapeDtypeStruct((FRAMES, DEPTH_DIM), jnp.float32),
            pltpu.HBM(ACTS, jnp.bfloat16),
            jax.ShapeDtypeStruct((FRAMES, 2), jnp.float32),
            pltpu.VMEM((2, FRAMES, DEPTH_DIM), jnp.bfloat16),
            pltpu.VMEM((2, DEPTH_DIM, VOCAB), jnp.bfloat16),
        ),
        in_specs=[SMEM] + [VMEM] * 4 + [HBM] * 3,
        out_specs=(VMEM, HBM, VMEM, VMEM, VMEM),
        scratch_shapes=[
            pltpu.VMEM(ACTS, jnp.bfloat16),
            pltpu.VMEM((FEATURES, DEPTH_DIM), jnp.bfloat16),
            pltpu.VMEM((2, FRAMES, DEPTH_DIM), jnp.bfloat16),
            pltpu.VMEM((2, DEPTH_DIM, VOCAB), jnp.bfloat16),
            pltpu.SemaphoreType.DMA((SEQ,)),
            pltpu.SemaphoreType.DMA((2, 2)),
            pltpu.SemaphoreType.DMA((2, 2)),
            pltpu.SemaphoreType.DMA((2, 2)),
        ],
        compiler_params=pltpu.CompilerParams(vmem_limit_bytes=DEPTH_GRANT),
        cost_estimate=DEPTH_COST,
    )(books, context, *small, depth_in, looked, heads)


def depth_second(book, projected, embed, heads, small):
    return pl.pallas_call(
        second_kernel,
        out_shape=(
            jax.ShapeDtypeStruct(ACTS, jnp.bfloat16),
            jax.ShapeDtypeStruct((FRAMES, 2), jnp.float32),
        ),
        in_specs=[SMEM] + [VMEM] * 6,
        out_specs=(VMEM, VMEM),
        compiler_params=pltpu.CompilerParams(vmem_limit_bytes=DEPTH_GRANT),
        cost_estimate=DEPTH_COST,
    )(book.reshape(1), projected, embed, heads, *small)


def outer_kernel(mine, theirs, out_hbm, out, sems):
    chunk = 128
    stores = []
    for step in range(DEPTH_DIM // chunk):
        at = step * chunk
        both = []
        for j in range(2):
            total = None
            for acts in (mine, theirs):
                term = lax.dot_general(
                    acts[0, j, :, at : at + chunk],
                    acts[1, j],
                    (((0,), (0,)), ((), ())),
                    preferred_element_type=jnp.float32,
                )
                total = term if total is None else total + term
            both.append(total.reshape(chunk // 8, 8, VOCAB))
        here = slice(at // 8, (at + chunk) // 8)
        out[here] = jnp.concatenate(both, axis=1).astype(jnp.bfloat16)
        copy = pltpu.make_async_copy(out.at[here], out_hbm.at[here], sems.at[step])
        copy.start()
        stores.append(copy)
    for copy in stores:
        copy.wait()


def outer(mine, theirs):
    return pl.pallas_call(
        outer_kernel,
        out_shape=pltpu.HBM((SEQ * WIDE, 16, VOCAB), jnp.bfloat16),
        in_specs=[VMEM] * 2,
        out_specs=HBM,
        scratch_shapes=[
            pltpu.VMEM((SEQ * WIDE, 16, VOCAB), jnp.bfloat16),
            pltpu.SemaphoreType.DMA((8,)),
        ],
        compiler_params=pltpu.CompilerParams(vmem_limit_bytes=40 * 2**20),
        cost_estimate=pl.CostEstimate(
            flops=2 * 2 * 2 * FRAMES * DEPTH_DIM * VOCAB,
            bytes_accessed=8 * 2**20,
            transcendentals=0,
        ),
    )(mine, theirs)


def total_kernel(scale, shares_hbm, out, shares, sems):
    chips = SEQ * WIDE // 2
    step = chips // 16
    loads = [
        pltpu.make_async_copy(
            shares_hbm.at[i * step : (i + 1) * step],
            shares.at[i * step : (i + 1) * step],
            sems.at[i],
        )
        for i in range(16)
    ]
    for copy in loads:
        copy.start()
    acc = None
    for i in range(16):
        loads[i].wait()
        term = jnp.sum(shares[i * step : (i + 1) * step].astype(jnp.float32), axis=0)
        acc = term if acc is None else acc + term
    for book in range(CODEBOOKS):
        out[:, book] = acc[book // 2, 8 * (book % 2) : 8 * (book % 2) + 8, :] * scale


def total(shares, scale):
    chips = SEQ * WIDE // 2
    return pl.pallas_call(
        partial(total_kernel, scale),
        out_shape=jax.ShapeDtypeStruct((8, CODEBOOKS, VOCAB), jnp.float32),
        in_specs=[HBM],
        out_specs=VMEM,
        scratch_shapes=[
            pltpu.VMEM((chips, 2, 16, VOCAB), jnp.bfloat16),
            pltpu.SemaphoreType.DMA((16,)),
        ],
        compiler_params=pltpu.CompilerParams(vmem_limit_bytes=GRANT),
        cost_estimate=pl.CostEstimate(
            flops=chips * 32 * VOCAB, bytes_accessed=chips * 64 * VOCAB, transcendentals=0
        ),
    )(shares.reshape(chips, 2, 16, VOCAB))


def normalize(norm_gain, mixed_in):
    return (
        mixed_in
        * lax.rsqrt(jnp.mean(mixed_in * mixed_in, axis=-1, keepdims=True) + 1e-05)
        * norm_gain[:, None, :]
    )


def swap_wide(array, stride):
    return lax.ppermute(array, "wide", [(i, i ^ stride) for i in range(WIDE)])


def share_step(held, axis, stride):
    high = (lax.axis_index("wide") // stride) % 2 == 1
    low_part = lax.index_in_dim(held, 0, axis, keepdims=True)
    high_part = lax.index_in_dim(held, 1, axis, keepdims=True)
    kept = jnp.where(high, high_part, low_part)
    came = swap_wide(jnp.where(high, low_part, high_part), stride)
    return jnp.concatenate(
        (jnp.where(high, came, kept), jnp.where(high, kept, came)), axis=axis
    )


def by_distance(rows):
    index = jnp.arange(WIDE, dtype=jnp.int32)
    pick = index[:, None] == (index[None, :] ^ lax.axis_index("wide"))
    return jnp.sum(jnp.where(pick[:, :, None], rows[None], 0), axis=1)


def share_out(rows):
    sent = by_distance(rows).reshape(4, 4, rows.shape[1])
    first = jnp.stack([sent[0]] + [swap_wide(sent[k], 4 * k) for k in range(1, 4)])
    second = [first[:, 0]] + [swap_wide(first[:, k], k) for k in range(1, 4)]
    return by_distance(jnp.stack(second, axis=1).reshape(WIDE, rows.shape[1]))


def shards(
    queries, key_vectors, values, audio_codes, depth_in, code_embed, norm_gain, out_heads, out_bias
):
    core = lax.axis_index("wide") % 2
    packed = pack(queries, key_vectors, values)
    held, packed = lax.optimization_barrier((audio_codes, packed))
    held = share_step(held.reshape(2, 2, 2, 2, 64), 0, 8)
    held = share_step(held, 1, 4)
    qkv = lax.all_to_all(packed, "seq", 0, 0, tiled=True)
    heads = out_heads.transpose(1, 0, 2)
    held, qkv, heads = lax.optimization_barrier((held, qkv, heads))
    held = share_step(held, 2, 2)
    context = attend(qkv)
    held, context = lax.optimization_barrier((held, context))
    context = lax.all_to_all(context, "seq", 0, 0, tiled=True)
    held = share_step(held, 3, 1)
    targets = held.reshape(FRAMES, CODEBOOKS)
    small = (norm_gain[:, None, :], out_bias[:, None, :], targets)
    mine = 2 * core
    other = 2 - mine
    looked = lookup(targets, code_embed)
    projected, acts_other, losses_other, *staged = depth_first(
        jnp.stack([other, mine]), context, small, depth_in, pltpu.with_memory_space_constraint(looked, pltpu.HBM), heads
    )
    came = swap_wide(acts_other, 1)
    acts_mine, losses_mine = depth_second(mine, projected, *staged, small)
    shares = lax.all_to_all(outer(acts_mine, came), ("seq", "wide"), 0, 0, tiled=True)
    grad_scale = (VOCAB / (SEQ * WIDE * FRAMES)) ** 0.5
    head_grads = total(shares, grad_scale)

    def in_order(of_mine, of_other):
        low = jnp.where(core == 0, of_mine, of_other)
        high = jnp.where(core == 0, of_other, of_mine)
        return jnp.concatenate((low, high), axis=0)

    dlogits = in_order(acts_mine[1], acts_other[1])
    pullback = jax.vjp(
        partial(normalize, norm_gain), projected[None] + looked.astype(jnp.float32)
    )[1]
    dhidden = jnp.einsum("cnv,cev->cne", dlogits, heads, preferred_element_type=jnp.float32)
    dmixed = pullback(dhidden)[0]
    dprojected = jnp.sum(dmixed, axis=0).astype(jnp.bfloat16)
    context_grad = lax.dot_general(
        dprojected, depth_in, (((1,), (1,)), ((), ())), preferred_element_type=jnp.float32
    ).astype(jnp.bfloat16)
    losses = jnp.where(
        core == 0,
        jnp.concatenate((losses_mine, losses_other), axis=1),
        jnp.concatenate((losses_other, losses_mine), axis=1),
    )
    losses, context_grad = lax.optimization_barrier((losses, context_grad))
    frame_losses = share_out(losses.reshape(WIDE, 64)).reshape(WIDE, 16, CODEBOOKS)
    return (frame_losses, context_grad.reshape(1, FRAMES, FEATURES), head_grads)


def solution(mesh):
    return jax.shard_map(
        shards,
        mesh=mesh,
        in_specs=(
            P("wide", "seq", None),
            P("wide", "seq", None),
            P("wide", "seq", None),
            P(None, ("seq", "wide"), None),
            P(),
            P(),
            P(),
            P(),
            P(),
        ),
        out_specs=(
            P(None, ("seq", "wide"), None),
            P("wide", "seq", None),
            P(("seq", "wide"), None, None),
        ),
        check_vma=False,
    )
```

```python
from functools import partial

import jax
import jax.numpy as jnp
from jax import lax
from jax.experimental import pallas as pl
from jax.experimental.pallas import tpu as pltpu
from jax.sharding import PartitionSpec as P

HEADS = 16
HEAD_DIM = 128
FEATURES = 2048
DEPTH_DIM = 1024
CODEBOOKS = 4
VOCAB = 1024
SEQ = 8
WIDE = 16
FRAMES = 256
LENGTH = SEQ * FRAMES
PAIR = 2 * HEAD_DIM


def attend_kernel(qkv, out_hbm, out, out_sems):
    stores = [
        pltpu.make_async_copy(out.at[i], out_hbm.at[i], out_sems.at[i]) for i in range(SEQ)
    ]
    to_exp2 = HEAD_DIM ** (-0.5) * 1.4426950408889634
    row = lax.broadcasted_iota(jnp.int32, (FRAMES, FRAMES), 0)
    col = lax.broadcasted_iota(jnp.int32, (FRAMES, FRAMES), 1)
    across = (((1,), (1,)), ((), ()))
    ones = jnp.ones((LENGTH, HEAD_DIM), jnp.bfloat16)

    def scores(block, head):
        at = head * HEAD_DIM
        q = qkv[block, :, at : at + HEAD_DIM]
        diag = lax.dot_general(
            q,
            qkv[block, :, PAIR + at : PAIR + at + HEAD_DIM],
            across,
            preferred_element_type=jnp.float32,
        )
        if not block:
            return (diag,)
        keys = qkv[:block, :, PAIR + at : PAIR + at + HEAD_DIM]
        past = lax.dot_general(
            q,
            keys.reshape(block * FRAMES, HEAD_DIM),
            across,
            preferred_element_type=jnp.float32,
        )
        return (diag, past)

    def combine(block, head, parts):
        at = 2 * PAIR + head * HEAD_DIM
        parts = (jnp.where(col <= row, parts[0], -jnp.inf),) + parts[1:]
        tops = [jnp.max(part, axis=1, keepdims=True) for part in parts]
        top = tops[0] if not block else jnp.maximum(*tops)
        acc = None
        for part, first, last in zip(parts, (block, 0), (block + 1, block)):
            weights = jnp.exp2((part - top) * to_exp2).astype(jnp.bfloat16)
            vals = qkv[first:last, :, at : at + HEAD_DIM].reshape(-1, HEAD_DIM)
            vals = jnp.concatenate((vals, ones[: vals.shape[0]]), axis=1)
            term = jnp.dot(weights, vals, preferred_element_type=jnp.float32)
            acc = term if acc is None else acc + term
        out[block, :, head * HEAD_DIM : (head + 1) * HEAD_DIM] = (
            acc[:, :HEAD_DIM] / acc[:, HEAD_DIM:]
        ).astype(jnp.bfloat16)

    tasks = [(block, head) for block in range(SEQ) for head in range(2)]
    present = scores(*tasks[0])
    for i, (block, head) in enumerate(tasks):
        following = scores(*tasks[i + 1]) if i + 1 < len(tasks) else None
        combine(block, head, present)
        present = following
        if head == 1:
            stores[block].start()
    for copy in stores:
        copy.wait()


HBM = pl.BlockSpec(memory_space=pltpu.HBM)
VMEM = pl.BlockSpec(memory_space=pltpu.VMEM)
SMEM = pl.BlockSpec(memory_space=pltpu.SMEM)
GRANT = 60 * 2**20
DEPTH_GRANT = 44 * 2**20


def attend(qkv):
    return pl.pallas_call(
        attend_kernel,
        out_shape=pltpu.HBM((SEQ, FRAMES, PAIR), jnp.bfloat16),
        in_specs=[VMEM],
        out_specs=HBM,
        scratch_shapes=[
            pltpu.VMEM((SEQ, FRAMES, PAIR), jnp.bfloat16),
            pltpu.SemaphoreType.DMA((SEQ,)),
        ],
        compiler_params=pltpu.CompilerParams(vmem_limit_bytes=40 * 2**20),
        cost_estimate=pl.CostEstimate(
            flops=2 * 36 * FRAMES * FRAMES * HEAD_DIM * 4,
            bytes_accessed=LENGTH * PAIR * 8,
            transcendentals=2 * 36 * FRAMES * FRAMES,
        ),
    )(qkv)


def pack_kernel(queries, key_vectors, values, out, held, in_sems, out_sems):
    rows = FRAMES // 4
    sources = (queries, key_vectors, values)
    loads = [
        [
            pltpu.make_async_copy(
                ref.at[0, i * rows : (i + 1) * rows],
                held.at[kind, i * rows : (i + 1) * rows],
                in_sems.at[i, kind],
            )
            for kind, ref in enumerate(sources)
        ]
        for i in range(4)
    ]
    for group in loads:
        for copy in group:
            copy.start()
    stores = []
    for i in range(4):
        for kind in range(3):
            loads[i][kind].wait()
            for part in range(SEQ):
                copy = pltpu.make_async_copy(
                    held.at[kind, i * rows : (i + 1) * rows, part * PAIR : (part + 1) * PAIR],
                    out.at[part, i * rows : (i + 1) * rows, kind * PAIR : (kind + 1) * PAIR],
                    out_sems.at[i, kind, part],
                )
                copy.start()
                stores.append(copy)
    for copy in stores:
        copy.wait()


def pack(queries, key_vectors, values):
    return pl.pallas_call(
        pack_kernel,
        out_shape=pltpu.HBM((SEQ, FRAMES, 3 * PAIR), jnp.bfloat16),
        in_specs=[HBM] * 3,
        out_specs=HBM,
        scratch_shapes=[
            pltpu.VMEM((3, FRAMES, FEATURES), jnp.bfloat16),
            pltpu.SemaphoreType.DMA((4, 3)),
            pltpu.SemaphoreType.DMA((4, 3, SEQ)),
        ],
        compiler_params=pltpu.CompilerParams(vmem_limit_bytes=GRANT),
        cost_estimate=pl.CostEstimate(flops=0, bytes_accessed=6 * 2**20, transcendentals=0),
    )(queries, key_vectors, values)


def lookup_kernel(target, table_hbm, looked_hbm, table, out, in_sems, out_sems):
    books = CODEBOOKS - 1
    loads = [
        pltpu.make_async_copy(table_hbm.at[c], table.at[c], in_sems.at[c]) for c in range(books)
    ]
    stores = [
        pltpu.make_async_copy(out.at[c], looked_hbm.at[c], out_sems.at[c])
        for c in range(CODEBOOKS)
    ]
    for copy in loads:
        copy.start()
    out[0] = jnp.zeros((FRAMES, DEPTH_DIM), jnp.bfloat16)
    stores[0].start()
    for c in range(books):
        loads[c].wait()
        chosen = lax.broadcasted_iota(jnp.int32, (FRAMES, VOCAB), 1) == target[:, c : c + 1]
        out[c + 1] = jnp.dot(
            chosen.astype(jnp.float32).astype(jnp.bfloat16),
            table[c],
            preferred_element_type=jnp.float32,
        ).astype(jnp.bfloat16)
        stores[c + 1].start()
    for copy in stores:
        copy.wait()


def lookup(target, table):
    return pl.pallas_call(
        lookup_kernel,
        out_shape=pltpu.HBM((CODEBOOKS, FRAMES, DEPTH_DIM), jnp.bfloat16),
        in_specs=[VMEM, HBM],
        out_specs=HBM,
        scratch_shapes=[
            pltpu.VMEM((CODEBOOKS - 1, VOCAB, DEPTH_DIM), jnp.bfloat16),
            pltpu.VMEM((CODEBOOKS, FRAMES, DEPTH_DIM), jnp.bfloat16),
            pltpu.SemaphoreType.DMA((CODEBOOKS - 1,)),
            pltpu.SemaphoreType.DMA((CODEBOOKS,)),
        ],
        compiler_params=pltpu.CompilerParams(vmem_limit_bytes=GRANT),
        cost_estimate=pl.CostEstimate(
            flops=6 * FRAMES * VOCAB * DEPTH_DIM, bytes_accessed=10 * 2**20, transcendentals=0
        ),
    )(target, table)


def depth_head(projected, embed, gain, heads, bias, target, keep):
    mixed = projected + embed.astype(jnp.float32)
    scale = lax.rsqrt(jnp.mean(mixed * mixed, axis=1, keepdims=True) + 1e-05)
    hidden = (mixed * scale * gain).astype(jnp.bfloat16)
    keep(hidden)
    logits = jnp.dot(hidden, heads, preferred_element_type=jnp.float32) + bias
    top = jnp.max(logits, axis=1, keepdims=True)
    shifted = jnp.exp(logits - top)
    total = jnp.sum(shifted, axis=1, keepdims=True)
    onehot = lax.broadcasted_iota(jnp.int32, (FRAMES, VOCAB), 1) == target
    picked = jnp.sum(jnp.where(onehot, logits, 0.0), axis=1, keepdims=True)
    losses = top + jnp.log(total) - picked
    dlogits = (shifted / total - onehot.astype(jnp.float32)).astype(jnp.bfloat16)
    return dlogits, losses


def depth_pair(
    book, projected, embed, heads, gain, bias, target, acts, losses, begin=None, finish=None
):
    lane = lax.broadcasted_iota(jnp.int32, (FRAMES, CODEBOOKS), 1)
    both = []
    for j in range(2):
        c = book[0] + j
        if begin:
            begin(j)
        token = jnp.sum(jnp.where(lane == c, target[...], 0), axis=1, keepdims=True)

        def keep(kind, value, j=j):
            acts[kind, j] = value
            if finish:
                finish(kind, j)

        dlogits, loss = depth_head(
            projected[...], embed[j], gain[c], heads[j], bias[c], token, partial(keep, 0)
        )
        keep(1, dlogits)
        both.append(loss)
    pair_lane = lax.broadcasted_iota(jnp.int32, (FRAMES, 2), 1)
    losses[...] = jnp.where(pair_lane == 0, both[0], both[1])


def first_kernel(
    book,
    ctx,
    gain,
    bias,
    target,
    depth_hbm,
    looked_hbm,
    heads_hbm,
    projected,
    acts_hbm,
    losses,
    next_embed,
    next_heads,
    acts,
    depth_in,
    embed,
    heads,
    depth_sems,
    book_sems,
    next_sems,
    out_sems,
):
    rows = [slice(part * PAIR, (part + 1) * PAIR) for part in range(SEQ)]
    depth_copies = [
        pltpu.make_async_copy(depth_hbm.at[rows[part]], depth_in.at[rows[part]], depth_sems.at[part])
        for part in range(SEQ)
    ]
    book_copies = [
        [
            pltpu.make_async_copy(looked_hbm.at[book[0] + j], embed.at[j], book_sems.at[0, j]),
            pltpu.make_async_copy(heads_hbm.at[book[0] + j], heads.at[j], book_sems.at[1, j]),
        ]
        for j in range(2)
    ]
    staged = []
    for j in range(2):
        c = book[1] + j
        staged.append(
            pltpu.make_async_copy(looked_hbm.at[c], next_embed.at[j], next_sems.at[0, j])
        )
        staged.append(
            pltpu.make_async_copy(heads_hbm.at[c], next_heads.at[j], next_sems.at[1, j])
        )
    for copy in depth_copies + book_copies[0]:
        copy.start()
    total = None
    for part in range(SEQ):
        depth_copies[part].wait()
        if part == SEQ // 2:
            for copy in book_copies[1]:
                copy.start()
        term = jnp.dot(ctx[part], depth_in[rows[part]], preferred_element_type=jnp.float32)
        total = term if total is None else total + term
    projected[...] = total
    for copy in staged:
        copy.start()
    stores = [
        [
            pltpu.make_async_copy(acts.at[kind, j], acts_hbm.at[kind, j], out_sems.at[kind, j])
            for kind in range(2)
        ]
        for j in range(2)
    ]

    def begin(j):
        for copy in book_copies[j]:
            copy.wait()

    def finish(kind, j):
        stores[j][kind].start()

    depth_pair(book, projected, embed, heads, gain, bias, target, acts, losses, begin, finish)
    for copy in staged + stores[0] + stores[1]:
        copy.wait()


def second_kernel(book, projected, embed, heads, gain, bias, target, acts, losses):
    depth_pair(book, projected, embed, heads, gain, bias, target, acts, losses)


DEPTH_COST = pl.CostEstimate(
    flops=2 * 2 * FRAMES * DEPTH_DIM * VOCAB,
    bytes_accessed=8 * 2**20,
    transcendentals=2 * FRAMES * VOCAB,
)
ACTS = (2, 2, FRAMES, DEPTH_DIM)


def depth_first(books, context, small, depth_in, looked, heads):
    return pl.pallas_call(
        first_kernel,
        out_shape=(
            jax.ShapeDtypeStruct((FRAMES, DEPTH_DIM), jnp.float32),
            pltpu.HBM(ACTS, jnp.bfloat16),
            jax.ShapeDtypeStruct((FRAMES, 2), jnp.float32),
            pltpu.VMEM((2, FRAMES, DEPTH_DIM), jnp.bfloat16),
            pltpu.VMEM((2, DEPTH_DIM, VOCAB), jnp.bfloat16),
        ),
        in_specs=[SMEM] + [VMEM] * 4 + [HBM] * 3,
        out_specs=(VMEM, HBM, VMEM, VMEM, VMEM),
        scratch_shapes=[
            pltpu.VMEM(ACTS, jnp.bfloat16),
            pltpu.VMEM((FEATURES, DEPTH_DIM), jnp.bfloat16),
            pltpu.VMEM((2, FRAMES, DEPTH_DIM), jnp.bfloat16),
            pltpu.VMEM((2, DEPTH_DIM, VOCAB), jnp.bfloat16),
            pltpu.SemaphoreType.DMA((SEQ,)),
            pltpu.SemaphoreType.DMA((2, 2)),
            pltpu.SemaphoreType.DMA((2, 2)),
            pltpu.SemaphoreType.DMA((2, 2)),
        ],
        compiler_params=pltpu.CompilerParams(vmem_limit_bytes=DEPTH_GRANT),
        cost_estimate=DEPTH_COST,
    )(books, context, *small, depth_in, looked, heads)


def depth_second(book, projected, embed, heads, small):
    return pl.pallas_call(
        second_kernel,
        out_shape=(
            jax.ShapeDtypeStruct(ACTS, jnp.bfloat16),
            jax.ShapeDtypeStruct((FRAMES, 2), jnp.float32),
        ),
        in_specs=[SMEM] + [VMEM] * 6,
        out_specs=(VMEM, VMEM),
        compiler_params=pltpu.CompilerParams(vmem_limit_bytes=DEPTH_GRANT),
        cost_estimate=DEPTH_COST,
    )(book.reshape(1), projected, embed, heads, *small)


def outer_kernel(mine, theirs, out_hbm, out, sems):
    chunk = 128
    stores = []
    for step in range(DEPTH_DIM // chunk):
        at = step * chunk
        both = []
        for j in range(2):
            total = None
            for acts in (mine, theirs):
                term = lax.dot_general(
                    acts[0, j, :, at : at + chunk],
                    acts[1, j],
                    (((0,), (0,)), ((), ())),
                    preferred_element_type=jnp.float32,
                )
                total = term if total is None else total + term
            both.append(total.reshape(chunk // 8, 8, VOCAB))
        here = slice(at // 8, (at + chunk) // 8)
        out[here] = jnp.concatenate(both, axis=1).astype(jnp.bfloat16)
        copy = pltpu.make_async_copy(out.at[here], out_hbm.at[here], sems.at[step])
        copy.start()
        stores.append(copy)
    for copy in stores:
        copy.wait()


def outer(mine, theirs):
    return pl.pallas_call(
        outer_kernel,
        out_shape=pltpu.HBM((SEQ * WIDE, 16, VOCAB), jnp.bfloat16),
        in_specs=[VMEM] * 2,
        out_specs=HBM,
        scratch_shapes=[
            pltpu.VMEM((SEQ * WIDE, 16, VOCAB), jnp.bfloat16),
            pltpu.SemaphoreType.DMA((8,)),
        ],
        compiler_params=pltpu.CompilerParams(vmem_limit_bytes=40 * 2**20),
        cost_estimate=pl.CostEstimate(
            flops=2 * 2 * 2 * FRAMES * DEPTH_DIM * VOCAB,
            bytes_accessed=8 * 2**20,
            transcendentals=0,
        ),
    )(mine, theirs)


def total_kernel(scale, shares_hbm, out, shares, sems):
    chips = SEQ * WIDE // 2
    step = chips // 16
    loads = [
        pltpu.make_async_copy(
            shares_hbm.at[i * step : (i + 1) * step],
            shares.at[i * step : (i + 1) * step],
            sems.at[i],
        )
        for i in range(16)
    ]
    for copy in loads:
        copy.start()
    acc = None
    for i in range(16):
        loads[i].wait()
        term = jnp.sum(shares[i * step : (i + 1) * step].astype(jnp.float32), axis=0)
        acc = term if acc is None else acc + term
    for book in range(CODEBOOKS):
        out[:, book] = acc[book // 2, 8 * (book % 2) : 8 * (book % 2) + 8, :] * scale


def total(shares, scale):
    chips = SEQ * WIDE // 2
    return pl.pallas_call(
        partial(total_kernel, scale),
        out_shape=jax.ShapeDtypeStruct((8, CODEBOOKS, VOCAB), jnp.float32),
        in_specs=[HBM],
        out_specs=VMEM,
        scratch_shapes=[
            pltpu.VMEM((chips, 2, 16, VOCAB), jnp.bfloat16),
            pltpu.SemaphoreType.DMA((16,)),
        ],
        compiler_params=pltpu.CompilerParams(vmem_limit_bytes=GRANT),
        cost_estimate=pl.CostEstimate(
            flops=chips * 32 * VOCAB, bytes_accessed=chips * 64 * VOCAB, transcendentals=0
        ),
    )(shares.reshape(chips, 2, 16, VOCAB))


def normalize(norm_gain, mixed_in):
    return (
        mixed_in
        * lax.rsqrt(jnp.mean(mixed_in * mixed_in, axis=-1, keepdims=True) + 1e-05)
        * norm_gain[:, None, :]
    )


def swap_wide(array, stride):
    return lax.ppermute(array, "wide", [(i, i ^ stride) for i in range(WIDE)])


def share_step(held, axis, stride):
    high = (lax.axis_index("wide") // stride) % 2 == 1
    low_part = lax.index_in_dim(held, 0, axis, keepdims=True)
    high_part = lax.index_in_dim(held, 1, axis, keepdims=True)
    kept = jnp.where(high, high_part, low_part)
    came = swap_wide(jnp.where(high, low_part, high_part), stride)
    return jnp.concatenate(
        (jnp.where(high, came, kept), jnp.where(high, kept, came)), axis=axis
    )


def by_distance(rows):
    index = jnp.arange(WIDE, dtype=jnp.int32)
    pick = index[:, None] == (index[None, :] ^ lax.axis_index("wide"))
    return jnp.sum(jnp.where(pick[:, :, None], rows[None], 0), axis=1)


def share_out(rows):
    sent = by_distance(rows).reshape(4, 4, rows.shape[1])
    first = jnp.stack([sent[0]] + [swap_wide(sent[k], 4 * k) for k in range(1, 4)])
    second = [first[:, 0]] + [swap_wide(first[:, k], k) for k in range(1, 4)]
    return by_distance(jnp.stack(second, axis=1).reshape(WIDE, rows.shape[1]))


def shards(
    queries, key_vectors, values, audio_codes, depth_in, code_embed, norm_gain, out_heads, out_bias
):
    core = lax.axis_index("wide") % 2
    packed = pack(queries, key_vectors, values)
    held, packed = lax.optimization_barrier((audio_codes, packed))
    held = share_step(held.reshape(2, 2, 2, 2, 64), 0, 8)
    held = share_step(held, 1, 4)
    qkv = lax.all_to_all(packed, "seq", 0, 0, tiled=True)
    heads = out_heads.transpose(1, 0, 2)
    held, qkv, heads = lax.optimization_barrier((held, qkv, heads))
    held = share_step(held, 2, 2)
    context = attend(qkv)
    held, context = lax.optimization_barrier((held, context))
    context = lax.all_to_all(context, "seq", 0, 0, tiled=True)
    held = share_step(held, 3, 1)
    targets = held.reshape(FRAMES, CODEBOOKS)
    small = (norm_gain[:, None, :], out_bias[:, None, :], targets)
    mine = 2 * core
    other = 2 - mine
    looked = lookup(targets, code_embed)
    projected, acts_other, losses_other, *staged = depth_first(
        jnp.stack([other, mine]), context, small, depth_in, pltpu.with_memory_space_constraint(looked, pltpu.HBM), heads
    )
    came = swap_wide(acts_other, 1)
    acts_mine, losses_mine = depth_second(mine, projected, *staged, small)
    shares = lax.all_to_all(outer(acts_mine, came), ("seq", "wide"), 0, 0, tiled=True)
    grad_scale = (VOCAB / (SEQ * WIDE * FRAMES)) ** 0.5
    head_grads = total(shares, grad_scale)

    def in_order(of_mine, of_other):
        low = jnp.where(core == 0, of_mine, of_other)
        high = jnp.where(core == 0, of_other, of_mine)
        return jnp.concatenate((low, high), axis=0)

    dlogits = in_order(acts_mine[1], acts_other[1])
    pullback = jax.vjp(
        partial(normalize, norm_gain), projected[None] + looked.astype(jnp.float32)
    )[1]
    dhidden = jnp.einsum("cnv,cev->cne", dlogits, heads, preferred_element_type=jnp.float32)
    dmixed = pullback(dhidden)[0]
    dprojected = jnp.sum(dmixed, axis=0).astype(jnp.bfloat16)
    context_grad = lax.dot_general(
        dprojected, depth_in, (((1,), (1,)), ((), ())), preferred_element_type=jnp.float32
    ).astype(jnp.bfloat16)
    losses = jnp.where(
        core == 0,
        jnp.concatenate((losses_mine, losses_other), axis=1),
        jnp.concatenate((losses_other, losses_mine), axis=1),
    )
    losses, context_grad = lax.optimization_barrier((losses, context_grad))
    frame_losses = share_out(losses.reshape(WIDE, 64)).reshape(WIDE, 16, CODEBOOKS)
    return (frame_losses, context_grad.reshape(1, FRAMES, FEATURES), head_grads)


def solution(mesh):
    return jax.shard_map(
        shards,
        mesh=mesh,
        in_specs=(
            P("wide", "seq", None),
            P("wide", "seq", None),
            P("wide", "seq", None),
            P(None, ("seq", "wide"), None),
            P(),
            P(),
            P(),
            P(),
            P(),
        ),
        out_specs=(
            P(None, ("seq", "wide"), None),
            P("wide", "seq", None),
            P(("seq", "wide"), None, None),
        ),
        check_vma=False,
    )
```

```python
from functools import partial

import jax
import jax.numpy as jnp
from jax import lax
from jax.experimental import pallas as pl
from jax.experimental.pallas import tpu as pltpu
from jax.sharding import PartitionSpec as P

HEADS = 16
HEAD_DIM = 128
FEATURES = 2048
DEPTH_DIM = 1024
CODEBOOKS = 4
VOCAB = 1024
SEQ = 8
WIDE = 16
FRAMES = 256
LENGTH = SEQ * FRAMES
PAIR = 2 * HEAD_DIM


def attend_kernel(qkv, out_hbm, out, out_sems):
    stores = [
        pltpu.make_async_copy(out.at[i], out_hbm.at[i], out_sems.at[i]) for i in range(SEQ)
    ]
    to_exp2 = HEAD_DIM ** (-0.5) * 1.4426950408889634
    row = lax.broadcasted_iota(jnp.int32, (FRAMES, FRAMES), 0)
    col = lax.broadcasted_iota(jnp.int32, (FRAMES, FRAMES), 1)
    across = (((1,), (1,)), ((), ()))
    ones = jnp.ones((LENGTH, HEAD_DIM), jnp.bfloat16)

    def scores(block, head):
        at = head * HEAD_DIM
        q = qkv[block, :, at : at + HEAD_DIM]
        diag = lax.dot_general(
            q,
            qkv[block, :, PAIR + at : PAIR + at + HEAD_DIM],
            across,
            preferred_element_type=jnp.float32,
        )
        if not block:
            return (diag,)
        keys = qkv[:block, :, PAIR + at : PAIR + at + HEAD_DIM]
        past = lax.dot_general(
            q,
            keys.reshape(block * FRAMES, HEAD_DIM),
            across,
            preferred_element_type=jnp.float32,
        )
        return (diag, past)

    def combine(block, head, parts):
        at = 2 * PAIR + head * HEAD_DIM
        parts = (jnp.where(col <= row, parts[0], -jnp.inf),) + parts[1:]
        tops = [jnp.max(part, axis=1, keepdims=True) for part in parts]
        top = tops[0] if not block else jnp.maximum(*tops)
        acc = None
        for part, first, last in zip(parts, (block, 0), (block + 1, block)):
            weights = jnp.exp2((part - top) * to_exp2).astype(jnp.bfloat16)
            vals = qkv[first:last, :, at : at + HEAD_DIM].reshape(-1, HEAD_DIM)
            vals = jnp.concatenate((vals, ones[: vals.shape[0]]), axis=1)
            term = jnp.dot(weights, vals, preferred_element_type=jnp.float32)
            acc = term if acc is None else acc + term
        out[block, :, head * HEAD_DIM : (head + 1) * HEAD_DIM] = (
            acc[:, :HEAD_DIM] / acc[:, HEAD_DIM:]
        ).astype(jnp.bfloat16)

    tasks = [(block, head) for block in range(SEQ) for head in range(2)]
    present = scores(*tasks[0])
    for i, (block, head) in enumerate(tasks):
        following = scores(*tasks[i + 1]) if i + 1 < len(tasks) else None
        combine(block, head, present)
        present = following
        if head == 1:
            stores[block].start()
    for copy in stores:
        copy.wait()


HBM = pl.BlockSpec(memory_space=pltpu.HBM)
VMEM = pl.BlockSpec(memory_space=pltpu.VMEM)
SMEM = pl.BlockSpec(memory_space=pltpu.SMEM)
GRANT = 60 * 2**20
DEPTH_GRANT = 44 * 2**20


def attend(qkv):
    return pl.pallas_call(
        attend_kernel,
        out_shape=pltpu.HBM((SEQ, FRAMES, PAIR), jnp.bfloat16),
        in_specs=[VMEM],
        out_specs=HBM,
        scratch_shapes=[
            pltpu.VMEM((SEQ, FRAMES, PAIR), jnp.bfloat16),
            pltpu.SemaphoreType.DMA((SEQ,)),
        ],
        compiler_params=pltpu.CompilerParams(vmem_limit_bytes=40 * 2**20),
        cost_estimate=pl.CostEstimate(
            flops=2 * 36 * FRAMES * FRAMES * HEAD_DIM * 4,
            bytes_accessed=LENGTH * PAIR * 8,
            transcendentals=2 * 36 * FRAMES * FRAMES,
        ),
    )(qkv)


def pack_kernel(queries, key_vectors, values, out, held, in_sems, out_sems):
    rows = FRAMES // 4
    sources = (queries, key_vectors, values)
    loads = [
        [
            pltpu.make_async_copy(
                ref.at[0, i * rows : (i + 1) * rows],
                held.at[kind, i * rows : (i + 1) * rows],
                in_sems.at[i, kind],
            )
            for kind, ref in enumerate(sources)
        ]
        for i in range(4)
    ]
    for group in loads:
        for copy in group:
            copy.start()
    stores = []
    for i in range(4):
        for kind in range(3):
            loads[i][kind].wait()
            for part in range(SEQ):
                copy = pltpu.make_async_copy(
                    held.at[kind, i * rows : (i + 1) * rows, part * PAIR : (part + 1) * PAIR],
                    out.at[part, i * rows : (i + 1) * rows, kind * PAIR : (kind + 1) * PAIR],
                    out_sems.at[i, kind, part],
                )
                copy.start()
                stores.append(copy)
    for copy in stores:
        copy.wait()


def pack(queries, key_vectors, values):
    return pl.pallas_call(
        pack_kernel,
        out_shape=pltpu.HBM((SEQ, FRAMES, 3 * PAIR), jnp.bfloat16),
        in_specs=[HBM] * 3,
        out_specs=HBM,
        scratch_shapes=[
            pltpu.VMEM((3, FRAMES, FEATURES), jnp.bfloat16),
            pltpu.SemaphoreType.DMA((4, 3)),
            pltpu.SemaphoreType.DMA((4, 3, SEQ)),
        ],
        compiler_params=pltpu.CompilerParams(vmem_limit_bytes=GRANT),
        cost_estimate=pl.CostEstimate(flops=0, bytes_accessed=6 * 2**20, transcendentals=0),
    )(queries, key_vectors, values)


def lookup_kernel(target, table_hbm, looked_hbm, table, out, in_sems, out_sems):
    books = CODEBOOKS - 1
    loads = [
        pltpu.make_async_copy(table_hbm.at[c], table.at[c], in_sems.at[c]) for c in range(books)
    ]
    stores = [
        pltpu.make_async_copy(out.at[c], looked_hbm.at[c], out_sems.at[c])
        for c in range(CODEBOOKS)
    ]
    for copy in loads:
        copy.start()
    out[0] = jnp.zeros((FRAMES, DEPTH_DIM), jnp.bfloat16)
    stores[0].start()
    for c in range(books):
        loads[c].wait()
        chosen = lax.broadcasted_iota(jnp.int32, (FRAMES, VOCAB), 1) == target[:, c : c + 1]
        out[c + 1] = jnp.dot(
            chosen.astype(jnp.float32).astype(jnp.bfloat16),
            table[c],
            preferred_element_type=jnp.float32,
        ).astype(jnp.bfloat16)
        stores[c + 1].start()
    for copy in stores:
        copy.wait()


def lookup(target, table):
    return pl.pallas_call(
        lookup_kernel,
        out_shape=pltpu.HBM((CODEBOOKS, FRAMES, DEPTH_DIM), jnp.bfloat16),
        in_specs=[VMEM, HBM],
        out_specs=HBM,
        scratch_shapes=[
            pltpu.VMEM((CODEBOOKS - 1, VOCAB, DEPTH_DIM), jnp.bfloat16),
            pltpu.VMEM((CODEBOOKS, FRAMES, DEPTH_DIM), jnp.bfloat16),
            pltpu.SemaphoreType.DMA((CODEBOOKS - 1,)),
            pltpu.SemaphoreType.DMA((CODEBOOKS,)),
        ],
        compiler_params=pltpu.CompilerParams(vmem_limit_bytes=GRANT),
        cost_estimate=pl.CostEstimate(
            flops=6 * FRAMES * VOCAB * DEPTH_DIM, bytes_accessed=10 * 2**20, transcendentals=0
        ),
    )(target, table)


def depth_head(projected, embed, gain, heads, bias, target, keep):
    mixed = projected + embed.astype(jnp.float32)
    scale = lax.rsqrt(jnp.mean(mixed * mixed, axis=1, keepdims=True) + 1e-05)
    hidden = (mixed * scale * gain).astype(jnp.bfloat16)
    keep(hidden)
    logits = jnp.dot(hidden, heads, preferred_element_type=jnp.float32) + bias
    top = jnp.max(logits, axis=1, keepdims=True)
    shifted = jnp.exp(logits - top)
    total = jnp.sum(shifted, axis=1, keepdims=True)
    onehot = lax.broadcasted_iota(jnp.int32, (FRAMES, VOCAB), 1) == target
    picked = jnp.sum(jnp.where(onehot, logits, 0.0), axis=1, keepdims=True)
    losses = top + jnp.log(total) - picked
    dlogits = (shifted / total - onehot.astype(jnp.float32)).astype(jnp.bfloat16)
    return dlogits, losses


def depth_pair(
    book, projected, embed, heads, gain, bias, target, acts, losses, begin=None, finish=None
):
    lane = lax.broadcasted_iota(jnp.int32, (FRAMES, CODEBOOKS), 1)
    both = []
    for j in range(2):
        c = book[0] + j
        if begin:
            begin(j)
        token = jnp.sum(jnp.where(lane == c, target[...], 0), axis=1, keepdims=True)

        def keep(kind, value, j=j):
            acts[kind, j] = value
            if finish:
                finish(kind, j)

        dlogits, loss = depth_head(
            projected[...], embed[j][...], gain[c], heads[j][...], bias[c], token, partial(keep, 0)
        )
        keep(1, dlogits)
        both.append(loss)
    pair_lane = lax.broadcasted_iota(jnp.int32, (FRAMES, 2), 1)
    losses[...] = jnp.where(pair_lane == 0, both[0], both[1])


def first_kernel(
    book,
    ctx,
    gain,
    bias,
    target,
    depth_hbm,
    looked_hbm,
    heads_hbm,
    projected,
    acts_hbm,
    losses,
    next_embed,
    next_heads,
    acts,
    depth_in,
    embed,
    heads,
    depth_sems,
    book_sems,
    next_sems,
    out_sems,
):
    rows = [slice(part * PAIR, (part + 1) * PAIR) for part in range(SEQ)]
    depth_copies = [
        pltpu.make_async_copy(depth_hbm.at[rows[part]], depth_in.at[rows[part]], depth_sems.at[part])
        for part in range(SEQ)
    ]
    book_copies = [
        [
            pltpu.make_async_copy(looked_hbm.at[book[0] + j], embed.at[j], book_sems.at[0, j]),
            pltpu.make_async_copy(heads_hbm.at[book[0] + j], heads.at[j], book_sems.at[1, j]),
        ]
        for j in range(2)
    ]
    staged = [
        pltpu.make_async_copy(looked_hbm.at[book[1]], next_embed, next_sems.at[0]),
        pltpu.make_async_copy(heads_hbm.at[book[1]], next_heads, next_sems.at[1]),
    ]
    for copy in depth_copies + book_copies[0]:
        copy.start()
    total = None
    for part in range(SEQ):
        depth_copies[part].wait()
        if part == SEQ // 2:
            for copy in book_copies[1]:
                copy.start()
        term = jnp.dot(ctx[part], depth_in[rows[part]], preferred_element_type=jnp.float32)
        total = term if total is None else total + term
    projected[...] = total
    for copy in staged:
        copy.start()
    stores = [
        [
            pltpu.make_async_copy(acts.at[kind, j], acts_hbm.at[kind, j], out_sems.at[kind, j])
            for kind in range(2)
        ]
        for j in range(2)
    ]

    def begin(j):
        for copy in book_copies[j]:
            copy.wait()

    def finish(kind, j):
        stores[j][kind].start()

    embed = (embed.at[0], embed.at[1])
    heads = (heads.at[0], heads.at[1])
    depth_pair(book, projected, embed, heads, gain, bias, target, acts, losses, begin, finish)
    for copy in staged + stores[0] + stores[1]:
        copy.wait()


def second_kernel(
    book,
    projected,
    first_embed,
    first_head,
    gain,
    bias,
    target,
    looked_hbm,
    heads_hbm,
    acts,
    losses,
    last_embed,
    last_head,
    sems,
):
    copies = [
        pltpu.make_async_copy(looked_hbm.at[book[0] + 1], last_embed, sems.at[0]),
        pltpu.make_async_copy(heads_hbm.at[book[0] + 1], last_head, sems.at[1]),
    ]
    for copy in copies:
        copy.start()

    def begin(j):
        if j:
            for copy in copies:
                copy.wait()

    embed = (first_embed, last_embed)
    heads = (first_head, last_head)
    depth_pair(book, projected, embed, heads, gain, bias, target, acts, losses, begin)


DEPTH_COST = pl.CostEstimate(
    flops=2 * 2 * FRAMES * DEPTH_DIM * VOCAB,
    bytes_accessed=8 * 2**20,
    transcendentals=2 * FRAMES * VOCAB,
)
ACTS = (2, 2, FRAMES, DEPTH_DIM)


def depth_first(books, context, small, depth_in, looked, heads):
    return pl.pallas_call(
        first_kernel,
        out_shape=(
            jax.ShapeDtypeStruct((FRAMES, DEPTH_DIM), jnp.float32),
            pltpu.HBM(ACTS, jnp.bfloat16),
            jax.ShapeDtypeStruct((FRAMES, 2), jnp.float32),
            pltpu.VMEM((FRAMES, DEPTH_DIM), jnp.bfloat16),
            pltpu.VMEM((DEPTH_DIM, VOCAB), jnp.bfloat16),
        ),
        in_specs=[SMEM] + [VMEM] * 4 + [HBM] * 3,
        out_specs=(VMEM, HBM, VMEM, VMEM, VMEM),
        scratch_shapes=[
            pltpu.VMEM(ACTS, jnp.bfloat16),
            pltpu.VMEM((FEATURES, DEPTH_DIM), jnp.bfloat16),
            pltpu.VMEM((2, FRAMES, DEPTH_DIM), jnp.bfloat16),
            pltpu.VMEM((2, DEPTH_DIM, VOCAB), jnp.bfloat16),
            pltpu.SemaphoreType.DMA((SEQ,)),
            pltpu.SemaphoreType.DMA((2, 2)),
            pltpu.SemaphoreType.DMA((2,)),
            pltpu.SemaphoreType.DMA((2, 2)),
        ],
        compiler_params=pltpu.CompilerParams(vmem_limit_bytes=DEPTH_GRANT),
        cost_estimate=DEPTH_COST,
    )(books, context, *small, depth_in, looked, heads)


def depth_second(book, projected, embed, head, small, looked, heads):
    return pl.pallas_call(
        second_kernel,
        out_shape=(
            jax.ShapeDtypeStruct(ACTS, jnp.bfloat16),
            jax.ShapeDtypeStruct((FRAMES, 2), jnp.float32),
        ),
        in_specs=[SMEM] + [VMEM] * 6 + [HBM] * 2,
        out_specs=(VMEM, VMEM),
        scratch_shapes=[
            pltpu.VMEM((FRAMES, DEPTH_DIM), jnp.bfloat16),
            pltpu.VMEM((DEPTH_DIM, VOCAB), jnp.bfloat16),
            pltpu.SemaphoreType.DMA((2,)),
        ],
        compiler_params=pltpu.CompilerParams(vmem_limit_bytes=DEPTH_GRANT),
        cost_estimate=DEPTH_COST,
    )(book.reshape(1), projected, embed, head, *small, looked, heads)


def outer_kernel(mine, theirs, out_hbm, out, sems):
    chunk = 128
    stores = []
    for step in range(DEPTH_DIM // chunk):
        at = step * chunk
        both = []
        for j in range(2):
            total = None
            for acts in (mine, theirs):
                term = lax.dot_general(
                    acts[0, j, :, at : at + chunk],
                    acts[1, j],
                    (((0,), (0,)), ((), ())),
                    preferred_element_type=jnp.float32,
                )
                total = term if total is None else total + term
            both.append(total.reshape(chunk // 8, 8, VOCAB))
        here = slice(at // 8, (at + chunk) // 8)
        out[here] = jnp.concatenate(both, axis=1).astype(jnp.bfloat16)
        copy = pltpu.make_async_copy(out.at[here], out_hbm.at[here], sems.at[step])
        copy.start()
        stores.append(copy)
    for copy in stores:
        copy.wait()


def outer(mine, theirs):
    return pl.pallas_call(
        outer_kernel,
        out_shape=pltpu.HBM((SEQ * WIDE, 16, VOCAB), jnp.bfloat16),
        in_specs=[VMEM] * 2,
        out_specs=HBM,
        scratch_shapes=[
            pltpu.VMEM((SEQ * WIDE, 16, VOCAB), jnp.bfloat16),
            pltpu.SemaphoreType.DMA((8,)),
        ],
        compiler_params=pltpu.CompilerParams(vmem_limit_bytes=40 * 2**20),
        cost_estimate=pl.CostEstimate(
            flops=2 * 2 * 2 * FRAMES * DEPTH_DIM * VOCAB,
            bytes_accessed=8 * 2**20,
            transcendentals=0,
        ),
    )(mine, theirs)


def total_kernel(scale, shares_hbm, out, shares, sems):
    chips = SEQ * WIDE // 2
    step = chips // 16
    loads = [
        pltpu.make_async_copy(
            shares_hbm.at[i * step : (i + 1) * step],
            shares.at[i * step : (i + 1) * step],
            sems.at[i],
        )
        for i in range(16)
    ]
    for copy in loads:
        copy.start()
    acc = None
    for i in range(16):
        loads[i].wait()
        term = jnp.sum(shares[i * step : (i + 1) * step].astype(jnp.float32), axis=0)
        acc = term if acc is None else acc + term
    for book in range(CODEBOOKS):
        out[:, book] = acc[book // 2, 8 * (book % 2) : 8 * (book % 2) + 8, :] * scale


def total(shares, scale):
    chips = SEQ * WIDE // 2
    return pl.pallas_call(
        partial(total_kernel, scale),
        out_shape=jax.ShapeDtypeStruct((8, CODEBOOKS, VOCAB), jnp.float32),
        in_specs=[HBM],
        out_specs=VMEM,
        scratch_shapes=[
            pltpu.VMEM((chips, 2, 16, VOCAB), jnp.bfloat16),
            pltpu.SemaphoreType.DMA((16,)),
        ],
        compiler_params=pltpu.CompilerParams(vmem_limit_bytes=GRANT),
        cost_estimate=pl.CostEstimate(
            flops=chips * 32 * VOCAB, bytes_accessed=chips * 64 * VOCAB, transcendentals=0
        ),
    )(shares.reshape(chips, 2, 16, VOCAB))


def normalize(norm_gain, mixed_in):
    return (
        mixed_in
        * lax.rsqrt(jnp.mean(mixed_in * mixed_in, axis=-1, keepdims=True) + 1e-05)
        * norm_gain[:, None, :]
    )


def swap_wide(array, stride):
    return lax.ppermute(array, "wide", [(i, i ^ stride) for i in range(WIDE)])


def share_step(held, axis, stride):
    high = (lax.axis_index("wide") // stride) % 2 == 1
    low_part = lax.index_in_dim(held, 0, axis, keepdims=True)
    high_part = lax.index_in_dim(held, 1, axis, keepdims=True)
    kept = jnp.where(high, high_part, low_part)
    came = swap_wide(jnp.where(high, low_part, high_part), stride)
    return jnp.concatenate(
        (jnp.where(high, came, kept), jnp.where(high, kept, came)), axis=axis
    )


def by_distance(rows):
    index = jnp.arange(WIDE, dtype=jnp.int32)
    pick = index[:, None] == (index[None, :] ^ lax.axis_index("wide"))
    return jnp.sum(jnp.where(pick[:, :, None], rows[None], 0), axis=1)


def share_out(rows):
    sent = by_distance(rows).reshape(4, 4, rows.shape[1])
    first = jnp.stack([sent[0]] + [swap_wide(sent[k], 4 * k) for k in range(1, 4)])
    second = [first[:, 0]] + [swap_wide(first[:, k], k) for k in range(1, 4)]
    return by_distance(jnp.stack(second, axis=1).reshape(WIDE, rows.shape[1]))


def shards(
    queries, key_vectors, values, audio_codes, depth_in, code_embed, norm_gain, out_heads, out_bias
):
    core = lax.axis_index("wide") % 2
    packed = pack(queries, key_vectors, values)
    held, packed = lax.optimization_barrier((audio_codes, packed))
    held = share_step(held.reshape(2, 2, 2, 2, 64), 0, 8)
    held = share_step(held, 1, 4)
    qkv = lax.all_to_all(packed, "seq", 0, 0, tiled=True)
    heads = out_heads.transpose(1, 0, 2)
    held, qkv, heads = lax.optimization_barrier((held, qkv, heads))
    held = share_step(held, 2, 2)
    context = attend(qkv)
    held, context = lax.optimization_barrier((held, context))
    context = lax.all_to_all(context, "seq", 0, 0, tiled=True)
    held = share_step(held, 3, 1)
    targets = held.reshape(FRAMES, CODEBOOKS)
    small = (norm_gain[:, None, :], out_bias[:, None, :], targets)
    mine = 2 * core
    other = 2 - mine
    looked = lookup(targets, code_embed)
    in_hbm = [pltpu.with_memory_space_constraint(a, pltpu.HBM) for a in (depth_in, looked, heads)]
    projected, acts_other, losses_other, *staged = depth_first(
        jnp.stack([other, mine]), context, small, *in_hbm
    )
    came = swap_wide(acts_other, 1)
    acts_mine, losses_mine = depth_second(mine, projected, *staged, small, *in_hbm[1:])
    shares = lax.all_to_all(outer(acts_mine, came), ("seq", "wide"), 0, 0, tiled=True)
    grad_scale = (VOCAB / (SEQ * WIDE * FRAMES)) ** 0.5
    head_grads = total(shares, grad_scale)

    def in_order(of_mine, of_other):
        low = jnp.where(core == 0, of_mine, of_other)
        high = jnp.where(core == 0, of_other, of_mine)
        return jnp.concatenate((low, high), axis=0)

    dlogits = in_order(acts_mine[1], acts_other[1])
    pullback = jax.vjp(
        partial(normalize, norm_gain), projected[None] + looked.astype(jnp.float32)
    )[1]
    dhidden = jnp.einsum("cnv,cev->cne", dlogits, heads, preferred_element_type=jnp.float32)
    dmixed = pullback(dhidden)[0]
    dprojected = jnp.sum(dmixed, axis=0).astype(jnp.bfloat16)
    context_grad = lax.dot_general(
        dprojected, depth_in, (((1,), (1,)), ((), ())), preferred_element_type=jnp.float32
    ).astype(jnp.bfloat16)
    losses = jnp.where(
        core == 0,
        jnp.concatenate((losses_mine, losses_other), axis=1),
        jnp.concatenate((losses_other, losses_mine), axis=1),
    )
    losses, context_grad = lax.optimization_barrier((losses, context_grad))
    frame_losses = share_out(losses.reshape(WIDE, 64)).reshape(WIDE, 16, CODEBOOKS)
    return (frame_losses, context_grad.reshape(1, FRAMES, FEATURES), head_grads)


def solution(mesh):
    return jax.shard_map(
        shards,
        mesh=mesh,
        in_specs=(
            P("wide", "seq", None),
            P("wide", "seq", None),
            P("wide", "seq", None),
            P(None, ("seq", "wide"), None),
            P(),
            P(),
            P(),
            P(),
            P(),
        ),
        out_specs=(
            P(None, ("seq", "wide"), None),
            P("wide", "seq", None),
            P(("seq", "wide"), None, None),
        ),
        check_vma=False,
    )
```

```python
from functools import partial

import jax
import jax.numpy as jnp
from jax import lax
from jax.experimental import pallas as pl
from jax.experimental.pallas import tpu as pltpu
from jax.sharding import PartitionSpec as P

HEADS = 16
HEAD_DIM = 128
FEATURES = 2048
DEPTH_DIM = 1024
CODEBOOKS = 4
VOCAB = 1024
SEQ = 8
WIDE = 16
FRAMES = 256
LENGTH = SEQ * FRAMES
PAIR = 2 * HEAD_DIM


def attend_kernel(qkv, out_hbm, out, out_sems):
    stores = [
        pltpu.make_async_copy(out.at[i], out_hbm.at[i], out_sems.at[i]) for i in range(SEQ)
    ]
    to_exp2 = HEAD_DIM ** (-0.5) * 1.4426950408889634
    row = lax.broadcasted_iota(jnp.int32, (FRAMES, FRAMES), 0)
    col = lax.broadcasted_iota(jnp.int32, (FRAMES, FRAMES), 1)
    across = (((1,), (1,)), ((), ()))
    ones = jnp.ones((LENGTH, HEAD_DIM), jnp.bfloat16)

    def scores(block, head):
        at = head * HEAD_DIM
        q = qkv[block, :, at : at + HEAD_DIM]
        diag = lax.dot_general(
            q,
            qkv[block, :, PAIR + at : PAIR + at + HEAD_DIM],
            across,
            preferred_element_type=jnp.float32,
        )
        if not block:
            return (diag,)
        keys = qkv[:block, :, PAIR + at : PAIR + at + HEAD_DIM]
        past = lax.dot_general(
            q,
            keys.reshape(block * FRAMES, HEAD_DIM),
            across,
            preferred_element_type=jnp.float32,
        )
        return (diag, past)

    def combine(block, head, parts):
        at = 2 * PAIR + head * HEAD_DIM
        parts = (jnp.where(col <= row, parts[0], -jnp.inf),) + parts[1:]
        tops = [jnp.max(part, axis=1, keepdims=True) for part in parts]
        top = tops[0] if not block else jnp.maximum(*tops)
        acc = None
        for part, first, last in zip(parts, (block, 0), (block + 1, block)):
            weights = jnp.exp2((part - top) * to_exp2).astype(jnp.bfloat16)
            vals = qkv[first:last, :, at : at + HEAD_DIM].reshape(-1, HEAD_DIM)
            vals = jnp.concatenate((vals, ones[: vals.shape[0]]), axis=1)
            term = jnp.dot(weights, vals, preferred_element_type=jnp.float32)
            acc = term if acc is None else acc + term
        out[block, :, head * HEAD_DIM : (head + 1) * HEAD_DIM] = (
            acc[:, :HEAD_DIM] / acc[:, HEAD_DIM:]
        ).astype(jnp.bfloat16)

    tasks = [(block, head) for block in range(SEQ) for head in range(2)]
    present = scores(*tasks[0])
    for i, (block, head) in enumerate(tasks):
        following = scores(*tasks[i + 1]) if i + 1 < len(tasks) else None
        combine(block, head, present)
        present = following
        if head == 1:
            stores[block].start()
    for copy in stores:
        copy.wait()


HBM = pl.BlockSpec(memory_space=pltpu.HBM)
VMEM = pl.BlockSpec(memory_space=pltpu.VMEM)
SMEM = pl.BlockSpec(memory_space=pltpu.SMEM)
GRANT = 60 * 2**20
DEPTH_GRANT = 44 * 2**20


def attend(qkv):
    return pl.pallas_call(
        attend_kernel,
        out_shape=pltpu.HBM((SEQ, FRAMES, PAIR), jnp.bfloat16),
        in_specs=[VMEM],
        out_specs=HBM,
        scratch_shapes=[
            pltpu.VMEM((SEQ, FRAMES, PAIR), jnp.bfloat16),
            pltpu.SemaphoreType.DMA((SEQ,)),
        ],
        compiler_params=pltpu.CompilerParams(vmem_limit_bytes=40 * 2**20),
        cost_estimate=pl.CostEstimate(
            flops=2 * 36 * FRAMES * FRAMES * HEAD_DIM * 4,
            bytes_accessed=LENGTH * PAIR * 8,
            transcendentals=2 * 36 * FRAMES * FRAMES,
        ),
    )(qkv)


def pack_kernel(queries, key_vectors, values, out, held, in_sems, out_sems):
    rows = FRAMES // 2
    sources = (queries, key_vectors, values)
    loads = [
        [
            pltpu.make_async_copy(
                ref.at[0, i * rows : (i + 1) * rows],
                held.at[kind, i * rows : (i + 1) * rows],
                in_sems.at[i, kind],
            )
            for kind, ref in enumerate(sources)
        ]
        for i in range(2)
    ]
    for group in loads:
        for copy in group:
            copy.start()
    stores = []
    for i in range(2):
        for kind in range(3):
            loads[i][kind].wait()
            for part in range(SEQ):
                copy = pltpu.make_async_copy(
                    held.at[kind, i * rows : (i + 1) * rows, part * PAIR : (part + 1) * PAIR],
                    out.at[part, i * rows : (i + 1) * rows, kind * PAIR : (kind + 1) * PAIR],
                    out_sems.at[i, kind, part],
                )
                copy.start()
                stores.append(copy)
    for copy in stores:
        copy.wait()


def pack(queries, key_vectors, values):
    return pl.pallas_call(
        pack_kernel,
        out_shape=pltpu.HBM((SEQ, FRAMES, 3 * PAIR), jnp.bfloat16),
        in_specs=[HBM] * 3,
        out_specs=HBM,
        scratch_shapes=[
            pltpu.VMEM((3, FRAMES, FEATURES), jnp.bfloat16),
            pltpu.SemaphoreType.DMA((2, 3)),
            pltpu.SemaphoreType.DMA((2, 3, SEQ)),
        ],
        compiler_params=pltpu.CompilerParams(vmem_limit_bytes=GRANT),
        cost_estimate=pl.CostEstimate(flops=0, bytes_accessed=6 * 2**20, transcendentals=0),
    )(queries, key_vectors, values)


def lookup_kernel(target, table_hbm, looked_hbm, table, out, in_sems, out_sems):
    books = CODEBOOKS - 1
    loads = [
        pltpu.make_async_copy(table_hbm.at[c], table.at[c], in_sems.at[c]) for c in range(books)
    ]
    stores = [
        pltpu.make_async_copy(out.at[c], looked_hbm.at[c], out_sems.at[c])
        for c in range(CODEBOOKS)
    ]
    for copy in loads:
        copy.start()
    out[0] = jnp.zeros((FRAMES, DEPTH_DIM), jnp.bfloat16)
    stores[0].start()
    for c in range(books):
        loads[c].wait()
        chosen = lax.broadcasted_iota(jnp.int32, (FRAMES, VOCAB), 1) == target[:, c : c + 1]
        out[c + 1] = jnp.dot(
            chosen.astype(jnp.float32).astype(jnp.bfloat16),
            table[c],
            preferred_element_type=jnp.float32,
        ).astype(jnp.bfloat16)
        stores[c + 1].start()
    for copy in stores:
        copy.wait()


def lookup(target, table):
    return pl.pallas_call(
        lookup_kernel,
        out_shape=pltpu.HBM((CODEBOOKS, FRAMES, DEPTH_DIM), jnp.bfloat16),
        in_specs=[VMEM, HBM],
        out_specs=HBM,
        scratch_shapes=[
            pltpu.VMEM((CODEBOOKS - 1, VOCAB, DEPTH_DIM), jnp.bfloat16),
            pltpu.VMEM((CODEBOOKS, FRAMES, DEPTH_DIM), jnp.bfloat16),
            pltpu.SemaphoreType.DMA((CODEBOOKS - 1,)),
            pltpu.SemaphoreType.DMA((CODEBOOKS,)),
        ],
        compiler_params=pltpu.CompilerParams(vmem_limit_bytes=GRANT),
        cost_estimate=pl.CostEstimate(
            flops=6 * FRAMES * VOCAB * DEPTH_DIM, bytes_accessed=10 * 2**20, transcendentals=0
        ),
    )(target, table)


def depth_head(projected, embed, gain, heads, bias, target, keep):
    mixed = projected + embed.astype(jnp.float32)
    scale = lax.rsqrt(jnp.mean(mixed * mixed, axis=1, keepdims=True) + 1e-05)
    hidden = (mixed * scale * gain).astype(jnp.bfloat16)
    keep(hidden)
    logits = jnp.dot(hidden, heads, preferred_element_type=jnp.float32) + bias
    top = jnp.max(logits, axis=1, keepdims=True)
    shifted = jnp.exp(logits - top)
    total = jnp.sum(shifted, axis=1, keepdims=True)
    onehot = lax.broadcasted_iota(jnp.int32, (FRAMES, VOCAB), 1) == target
    picked = jnp.sum(jnp.where(onehot, logits, 0.0), axis=1, keepdims=True)
    losses = top + jnp.log(total) - picked
    dlogits = (shifted / total - onehot.astype(jnp.float32)).astype(jnp.bfloat16)
    return dlogits, losses


def depth_pair(
    book, projected, embed, heads, gain, bias, target, acts, losses, begin=None, finish=None
):
    lane = lax.broadcasted_iota(jnp.int32, (FRAMES, CODEBOOKS), 1)
    both = []
    for j in range(2):
        c = book[0] + j
        if begin:
            begin(j)
        token = jnp.sum(jnp.where(lane == c, target[...], 0), axis=1, keepdims=True)

        def keep(kind, value, j=j):
            acts[kind, j] = value
            if finish:
                finish(kind, j)

        dlogits, loss = depth_head(
            projected[...], embed[j][...], gain[c], heads[j][...], bias[c], token, partial(keep, 0)
        )
        keep(1, dlogits)
        both.append(loss)
    pair_lane = lax.broadcasted_iota(jnp.int32, (FRAMES, 2), 1)
    losses[...] = jnp.where(pair_lane == 0, both[0], both[1])


def first_kernel(
    book,
    ctx,
    gain,
    bias,
    target,
    depth_hbm,
    looked_hbm,
    heads_hbm,
    projected,
    acts_hbm,
    losses,
    next_embed,
    next_heads,
    acts,
    depth_in,
    embed,
    heads,
    depth_sems,
    book_sems,
    next_sems,
    out_sems,
):
    rows = [slice(part * PAIR, (part + 1) * PAIR) for part in range(SEQ)]
    depth_copies = [
        pltpu.make_async_copy(depth_hbm.at[rows[part]], depth_in.at[rows[part]], depth_sems.at[part])
        for part in range(SEQ)
    ]
    book_copies = [
        [
            pltpu.make_async_copy(looked_hbm.at[book[0] + j], embed.at[j], book_sems.at[0, j]),
            pltpu.make_async_copy(heads_hbm.at[book[0] + j], heads.at[j], book_sems.at[1, j]),
        ]
        for j in range(2)
    ]
    staged = [
        pltpu.make_async_copy(looked_hbm.at[book[1]], next_embed, next_sems.at[0]),
        pltpu.make_async_copy(heads_hbm.at[book[1]], next_heads, next_sems.at[1]),
    ]
    for copy in depth_copies + book_copies[0]:
        copy.start()
    total = None
    for part in range(SEQ):
        depth_copies[part].wait()
        if part == SEQ // 2:
            for copy in book_copies[1]:
                copy.start()
        term = jnp.dot(ctx[part], depth_in[rows[part]], preferred_element_type=jnp.float32)
        total = term if total is None else total + term
    projected[...] = total
    for copy in staged:
        copy.start()
    stores = [
        [
            pltpu.make_async_copy(acts.at[kind, j], acts_hbm.at[kind, j], out_sems.at[kind, j])
            for kind in range(2)
        ]
        for j in range(2)
    ]

    def begin(j):
        for copy in book_copies[j]:
            copy.wait()

    def finish(kind, j):
        stores[j][kind].start()

    embed = (embed.at[0], embed.at[1])
    heads = (heads.at[0], heads.at[1])
    depth_pair(book, projected, embed, heads, gain, bias, target, acts, losses, begin, finish)
    for copy in staged + stores[0] + stores[1]:
        copy.wait()


def second_kernel(
    book,
    projected,
    first_embed,
    first_head,
    gain,
    bias,
    target,
    looked_hbm,
    heads_hbm,
    acts,
    losses,
    last_embed,
    last_head,
    sems,
):
    copies = [
        pltpu.make_async_copy(looked_hbm.at[book[0] + 1], last_embed, sems.at[0]),
        pltpu.make_async_copy(heads_hbm.at[book[0] + 1], last_head, sems.at[1]),
    ]
    for copy in copies:
        copy.start()

    def begin(j):
        if j:
            for copy in copies:
                copy.wait()

    embed = (first_embed, last_embed)
    heads = (first_head, last_head)
    depth_pair(book, projected, embed, heads, gain, bias, target, acts, losses, begin)


DEPTH_COST = pl.CostEstimate(
    flops=2 * 2 * FRAMES * DEPTH_DIM * VOCAB,
    bytes_accessed=8 * 2**20,
    transcendentals=2 * FRAMES * VOCAB,
)
ACTS = (2, 2, FRAMES, DEPTH_DIM)


def depth_first(books, context, small, depth_in, looked, heads):
    return pl.pallas_call(
        first_kernel,
        out_shape=(
            jax.ShapeDtypeStruct((FRAMES, DEPTH_DIM), jnp.float32),
            pltpu.HBM(ACTS, jnp.bfloat16),
            jax.ShapeDtypeStruct((FRAMES, 2), jnp.float32),
            pltpu.VMEM((FRAMES, DEPTH_DIM), jnp.bfloat16),
            pltpu.VMEM((DEPTH_DIM, VOCAB), jnp.bfloat16),
        ),
        in_specs=[SMEM] + [VMEM] * 4 + [HBM] * 3,
        out_specs=(VMEM, HBM, VMEM, VMEM, VMEM),
        scratch_shapes=[
            pltpu.VMEM(ACTS, jnp.bfloat16),
            pltpu.VMEM((FEATURES, DEPTH_DIM), jnp.bfloat16),
            pltpu.VMEM((2, FRAMES, DEPTH_DIM), jnp.bfloat16),
            pltpu.VMEM((2, DEPTH_DIM, VOCAB), jnp.bfloat16),
            pltpu.SemaphoreType.DMA((SEQ,)),
            pltpu.SemaphoreType.DMA((2, 2)),
            pltpu.SemaphoreType.DMA((2,)),
            pltpu.SemaphoreType.DMA((2, 2)),
        ],
        compiler_params=pltpu.CompilerParams(vmem_limit_bytes=DEPTH_GRANT),
        cost_estimate=DEPTH_COST,
    )(books, context, *small, depth_in, looked, heads)


def depth_second(book, projected, embed, head, small, looked, heads):
    return pl.pallas_call(
        second_kernel,
        out_shape=(
            jax.ShapeDtypeStruct(ACTS, jnp.bfloat16),
            jax.ShapeDtypeStruct((FRAMES, 2), jnp.float32),
        ),
        in_specs=[SMEM] + [VMEM] * 6 + [HBM] * 2,
        out_specs=(VMEM, VMEM),
        scratch_shapes=[
            pltpu.VMEM((FRAMES, DEPTH_DIM), jnp.bfloat16),
            pltpu.VMEM((DEPTH_DIM, VOCAB), jnp.bfloat16),
            pltpu.SemaphoreType.DMA((2,)),
        ],
        compiler_params=pltpu.CompilerParams(vmem_limit_bytes=DEPTH_GRANT),
        cost_estimate=DEPTH_COST,
    )(book.reshape(1), projected, embed, head, *small, looked, heads)


def outer_kernel(mine, theirs, out_hbm, out, sems):
    chunk = 128
    stores = []
    for step in range(DEPTH_DIM // chunk):
        at = step * chunk
        both = []
        for j in range(2):
            total = None
            for acts in (mine, theirs):
                term = lax.dot_general(
                    acts[0, j, :, at : at + chunk],
                    acts[1, j],
                    (((0,), (0,)), ((), ())),
                    preferred_element_type=jnp.float32,
                )
                total = term if total is None else total + term
            both.append(total.reshape(chunk // 8, 8, VOCAB))
        here = slice(at // 8, (at + chunk) // 8)
        out[here] = jnp.concatenate(both, axis=1).astype(jnp.bfloat16)
        copy = pltpu.make_async_copy(out.at[here], out_hbm.at[here], sems.at[step])
        copy.start()
        stores.append(copy)
    for copy in stores:
        copy.wait()


def outer(mine, theirs):
    return pl.pallas_call(
        outer_kernel,
        out_shape=pltpu.HBM((SEQ * WIDE, 16, VOCAB), jnp.bfloat16),
        in_specs=[VMEM] * 2,
        out_specs=HBM,
        scratch_shapes=[
            pltpu.VMEM((SEQ * WIDE, 16, VOCAB), jnp.bfloat16),
            pltpu.SemaphoreType.DMA((8,)),
        ],
        compiler_params=pltpu.CompilerParams(vmem_limit_bytes=40 * 2**20),
        cost_estimate=pl.CostEstimate(
            flops=2 * 2 * 2 * FRAMES * DEPTH_DIM * VOCAB,
            bytes_accessed=8 * 2**20,
            transcendentals=0,
        ),
    )(mine, theirs)


def total_kernel(scale, shares_hbm, out, shares, sems):
    chips = SEQ * WIDE // 2
    step = chips // 16
    loads = [
        pltpu.make_async_copy(
            shares_hbm.at[i * step : (i + 1) * step],
            shares.at[i * step : (i + 1) * step],
            sems.at[i],
        )
        for i in range(16)
    ]
    for copy in loads:
        copy.start()
    acc = None
    for i in range(16):
        loads[i].wait()
        term = jnp.sum(shares[i * step : (i + 1) * step].astype(jnp.float32), axis=0)
        acc = term if acc is None else acc + term
    for book in range(CODEBOOKS):
        out[:, book] = acc[book // 2, 8 * (book % 2) : 8 * (book % 2) + 8, :] * scale


def total(shares, scale):
    chips = SEQ * WIDE // 2
    return pl.pallas_call(
        partial(total_kernel, scale),
        out_shape=jax.ShapeDtypeStruct((8, CODEBOOKS, VOCAB), jnp.float32),
        in_specs=[HBM],
        out_specs=VMEM,
        scratch_shapes=[
            pltpu.VMEM((chips, 2, 16, VOCAB), jnp.bfloat16),
            pltpu.SemaphoreType.DMA((16,)),
        ],
        compiler_params=pltpu.CompilerParams(vmem_limit_bytes=GRANT),
        cost_estimate=pl.CostEstimate(
            flops=chips * 32 * VOCAB, bytes_accessed=chips * 64 * VOCAB, transcendentals=0
        ),
    )(shares.reshape(chips, 2, 16, VOCAB))


def normalize(norm_gain, mixed_in):
    return (
        mixed_in
        * lax.rsqrt(jnp.mean(mixed_in * mixed_in, axis=-1, keepdims=True) + 1e-05)
        * norm_gain[:, None, :]
    )


def swap_wide(array, stride):
    return lax.ppermute(array, "wide", [(i, i ^ stride) for i in range(WIDE)])


def share_step(held, axis, stride):
    high = (lax.axis_index("wide") // stride) % 2 == 1
    low_part = lax.index_in_dim(held, 0, axis, keepdims=True)
    high_part = lax.index_in_dim(held, 1, axis, keepdims=True)
    kept = jnp.where(high, high_part, low_part)
    came = swap_wide(jnp.where(high, low_part, high_part), stride)
    return jnp.concatenate(
        (jnp.where(high, came, kept), jnp.where(high, kept, came)), axis=axis
    )


def by_distance(rows):
    index = jnp.arange(WIDE, dtype=jnp.int32)
    pick = index[:, None] == (index[None, :] ^ lax.axis_index("wide"))
    return jnp.sum(jnp.where(pick[:, :, None], rows[None], 0), axis=1)


def share_out(rows):
    sent = by_distance(rows).reshape(4, 4, rows.shape[1])
    first = jnp.stack([sent[0]] + [swap_wide(sent[k], 4 * k) for k in range(1, 4)])
    second = [first[:, 0]] + [swap_wide(first[:, k], k) for k in range(1, 4)]
    return by_distance(jnp.stack(second, axis=1).reshape(WIDE, rows.shape[1]))


def shards(
    queries, key_vectors, values, audio_codes, depth_in, code_embed, norm_gain, out_heads, out_bias
):
    core = lax.axis_index("wide") % 2
    packed = pack(queries, key_vectors, values)
    held, packed = lax.optimization_barrier((audio_codes, packed))
    held = share_step(held.reshape(2, 2, 2, 2, 64), 0, 8)
    held = share_step(held, 1, 4)
    qkv = lax.all_to_all(packed, "seq", 0, 0, tiled=True)
    heads = out_heads.transpose(1, 0, 2)
    held, qkv, heads = lax.optimization_barrier((held, qkv, heads))
    held = share_step(held, 2, 2)
    context = attend(qkv)
    held, context = lax.optimization_barrier((held, context))
    context = lax.all_to_all(context, "seq", 0, 0, tiled=True)
    held = share_step(held, 3, 1)
    targets = held.reshape(FRAMES, CODEBOOKS)
    small = (norm_gain[:, None, :], out_bias[:, None, :], targets)
    mine = 2 * core
    other = 2 - mine
    looked = lookup(targets, code_embed)
    in_hbm = [pltpu.with_memory_space_constraint(a, pltpu.HBM) for a in (depth_in, looked, heads)]
    projected, acts_other, losses_other, *staged = depth_first(
        jnp.stack([other, mine]), context, small, *in_hbm
    )
    came = swap_wide(acts_other, 1)
    acts_mine, losses_mine = depth_second(mine, projected, *staged, small, *in_hbm[1:])
    shares = lax.all_to_all(outer(acts_mine, came), ("seq", "wide"), 0, 0, tiled=True)
    grad_scale = (VOCAB / (SEQ * WIDE * FRAMES)) ** 0.5
    head_grads = total(shares, grad_scale)

    def in_order(of_mine, of_other):
        low = jnp.where(core == 0, of_mine, of_other)
        high = jnp.where(core == 0, of_other, of_mine)
        return jnp.concatenate((low, high), axis=0)

    dlogits = in_order(acts_mine[1], acts_other[1])
    pullback = jax.vjp(
        partial(normalize, norm_gain), projected[None] + looked.astype(jnp.float32)
    )[1]
    dhidden = jnp.einsum("cnv,cev->cne", dlogits, heads, preferred_element_type=jnp.float32)
    dmixed = pullback(dhidden)[0]
    dprojected = jnp.sum(dmixed, axis=0).astype(jnp.bfloat16)
    context_grad = lax.dot_general(
        dprojected, depth_in, (((1,), (1,)), ((), ())), preferred_element_type=jnp.float32
    ).astype(jnp.bfloat16)
    losses = jnp.where(
        core == 0,
        jnp.concatenate((losses_mine, losses_other), axis=1),
        jnp.concatenate((losses_other, losses_mine), axis=1),
    )
    losses, context_grad = lax.optimization_barrier((losses, context_grad))
    frame_losses = share_out(losses.reshape(WIDE, 64)).reshape(WIDE, 16, CODEBOOKS)
    return (frame_losses, context_grad.reshape(1, FRAMES, FEATURES), head_grads)


def solution(mesh):
    return jax.shard_map(
        shards,
        mesh=mesh,
        in_specs=(
            P("wide", "seq", None),
            P("wide", "seq", None),
            P("wide", "seq", None),
            P(None, ("seq", "wide"), None),
            P(),
            P(),
            P(),
            P(),
            P(),
        ),
        out_specs=(
            P(None, ("seq", "wide"), None),
            P("wide", "seq", None),
            P(("seq", "wide"), None, None),
        ),
        check_vma=False,
    )
```
